512 devices in a mesh: dc: 64 (over y, x, core), tp: 8 (over z).
Axes of the slice: x: 4, y: 8, z: 8, core: 2. Of those that a mesh axis runs over, the one named last changes fastest.
Arguments:
- queries: bfloat16 [8192, 8192], P(('dc', 'tp')), may hold values from -10 to 10
- keys: bfloat16 [8192, 1024], P(('dc', 'tp')), may hold values from -4 to 4
- values: bfloat16 [8192, 1024], P(('dc', 'tp')), may hold values from -6 to 6
- document_index: int32 [8192], P('dc'), may hold values from 0 to 15, never falling along the last dimension, each value on 1 to 4096 neighbouring positions
- owner: int32 [8192], P('dc'), may hold values from 0 to 63, as said below
Outputs:
- attended: bfloat16 [8192, 8192], P('dc', 'tp')
The draws below stay inside these ranges and needn't reach their ends.
Inputs may be any that keep to these rules, and one draw needn't show every extreme that they name: Each owner 0 to 63 is named by exactly 128 rows; of one index's 128 rows at most 4 name the same owner, and in every draw some index sends exactly 4 rows to one owner.
All inputs are finite; a program needn't handle non-finite values.
Results may differ from the reference program's by a relative error of at most 0.0035.
Values may be sent and summed in bfloat16 or wider, within the bound.
A program may use at most 64 MiB of HBM per device.

```python
import math
import jax
import jax.numpy as jnp
import numpy as np
from jax import lax

HEADS = 64
KVH = 8
HEAD_DIM = 128
TOK_DEV = 128
TOKENS = 8192
DOCS = 16
DOC_MOST = 4096
N_DC = 64


def draw_queries(key, part):
    key = jax.random.fold_in(key, 11)
    result = jnp.clip(jax.random.normal(key, (TOKENS, HEADS * HEAD_DIM), jnp.float32), -4.0, 4.0)
    return result.astype(jnp.bfloat16)


def draw_keys(key, part):
    key = jax.random.fold_in(key, 12)
    result = jnp.clip(jax.random.normal(key, (TOKENS, KVH * HEAD_DIM), jnp.float32), -4.0, 4.0)
    return result.astype(jnp.bfloat16)


def draw_owner(key, part):
    key = jax.random.fold_in(key, 13)
    first, second, third = jax.random.split(key, 3)
    base_count = TOK_DEV // N_DC
    shift_one = jax.random.randint(first, (), 1, N_DC)
    shift_two = (shift_one + jax.random.randint(second, (), 1, N_DC - 1)) % N_DC
    sources = jnp.arange(N_DC, dtype=jnp.int32)[:, None]
    targets = jnp.arange(N_DC, dtype=jnp.int32)[None, :]
    counts = base_count + base_count * (targets == (sources + shift_one) % N_DC).astype(jnp.int32) - base_count * (targets == (sources + shift_two) % N_DC).astype(jnp.int32)

    def per_source(source_key, source_counts):
        permuted_rows = jax.random.permutation(source_key, TOK_DEV)
        listing = jnp.repeat(jnp.arange(N_DC, dtype=jnp.int32), source_counts, total_repeat_length=TOK_DEV)
        return jnp.zeros((TOK_DEV,), jnp.int32).at[permuted_rows].set(listing)
    source_keys = jax.random.split(third, N_DC)
    return jax.vmap(per_source)(source_keys, counts).reshape(TOKENS)


def shard_levels(rng, extent, pieces, low, high):
    level, own = 1.0, jax.random.fold_in(rng, 6)
    for dim, blocks in pieces:
        heights = jnp.exp(jax.random.uniform(jax.random.fold_in(own, dim), (blocks,), jnp.float32, low / len(pieces), high / len(pieces)))
        level = level * jnp.repeat(heights, extent[dim] // blocks).reshape([-1 if axis == dim else 1 for axis in range(len(extent))])
    return level


def length_profile(number_of, total, limit, lean):
    weights = [(1 << 20) // math.isqrt(rank ** lean) + 1 for rank in range(2, number_of + 1)]
    spare, given = total - limit - (number_of - 1), [1] * (number_of - 1)
    while spare > 0:
        free = [i for i in range(number_of - 1) if given[i] < limit]
        pool, left = sum([weights[i] for i in free]), spare
        for i in free:
            more = min(limit - given[i], max(1, left * weights[i] // pool), spare)
            given[i] = given[i] + more
            spare = spare - more
    return np.array([limit] + given)


def uneven_parts(key, amount, total, limit, slope):
    if amount == 2:
        one = jax.random.randint(key, (), max(1, total - limit), min(limit, total - 1) + 1)
        return jnp.stack([one, total - one])
    tallies = jnp.asarray(length_profile(amount, total, limit, slope), jnp.int32)
    couples = (amount - 1) // 2
    giver, sink = tallies[1:1 + 2 * couples:2], tallies[2:2 + 2 * couples:2]
    slack = jnp.minimum(giver - 1, limit - sink)
    passed = jax.random.randint(jax.random.fold_in(key, 1), (couples,), 0, 1 << 20) % (slack + 1)
    tallies = tallies.at[1:1 + 2 * couples:2].set(giver - passed).at[2:2 + 2 * couples:2].set(sink + passed)
    return tallies[jax.random.permutation(jax.random.fold_in(key, 2), amount)]


def normal_values(rng, dims, width, bound, pieces=(), kind=jnp.bfloat16):
    drawn = width * jax.random.normal(rng, dims, jnp.float32)
    if pieces:
        drawn = drawn * shard_levels(rng, dims, pieces, -0.22, 0.18)
    return jnp.clip(drawn, -bound, bound).astype(kind)


def setup_inputs(seed: int = 0) -> dict:
    arg_keys = jax.random.split(jax.random.key(seed), 6)
    return {
        "queries": draw_queries(jax.random.fold_in(arg_keys[5], 71), 0),
        "keys": draw_keys(jax.random.fold_in(arg_keys[5], 71), 0),
        "values": normal_values(arg_keys[2], (TOKENS, KVH * HEAD_DIM), 1.0, 6.0, ((0, 512),)),
        "document_index": jnp.searchsorted(jnp.cumsum(uneven_parts(arg_keys[3], DOCS, TOKENS, DOC_MOST, 2)), jnp.arange(TOKENS), side="right").astype(jnp.int32),
        "owner": draw_owner(jax.random.fold_in(arg_keys[5], 71), 0),
    }


def reference(queries, keys, values, document_index, owner):
    per_group = HEADS // KVH
    scaling = 1.0 / math.sqrt(HEAD_DIM)
    query_heads = queries.reshape(TOKENS, KVH, per_group, HEAD_DIM)
    key_heads = keys.reshape(TOKENS, KVH, HEAD_DIM).astype(jnp.float32)
    value_heads = values.reshape(TOKENS, KVH, HEAD_DIM).astype(jnp.float32)
    places = jnp.arange(TOKENS, dtype=jnp.int32)

    def one_block(number):
        offset = (number * TOK_DEV).astype(jnp.int32)
        query_block = lax.dynamic_slice_in_dim(query_heads, offset, TOK_DEV, 0).astype(jnp.float32)
        query_place = offset + jnp.arange(TOK_DEV, dtype=jnp.int32)
        query_doc = lax.dynamic_slice_in_dim(document_index, offset, TOK_DEV, 0)
        allowed = (document_index[None, :] == query_doc[:, None]) & (places[None, :] <= query_place[:, None])
        scores = jnp.einsum('rkgd,tkd->rkgt', query_block, key_heads) * scaling
        masked = jnp.where(allowed[:, None, None, :], scores, -1e+30)
        peak = lax.optimization_barrier(jnp.max(masked, axis=-1, keepdims=True))
        weights = jnp.where(allowed[:, None, None, :], jnp.exp(masked - peak), 0.0)
        total = lax.optimization_barrier(jnp.sum(weights, axis=-1))
        rounded = lax.optimization_barrier(weights.astype(jnp.bfloat16)).astype(jnp.float32)
        summed = jnp.einsum('rkgt,tkd->rkgd', rounded, value_heads)
        context = summed / total[..., None]
        return context.reshape(TOK_DEV, HEADS * HEAD_DIM).astype(jnp.bfloat16)
    context = lax.map(one_block, jnp.arange(TOKENS // TOK_DEV, dtype=jnp.int32))
    context = context.reshape(TOKENS, HEADS * HEAD_DIM)
    ordering = jnp.argsort(owner, stable=True)
    return context[ordering]
```

```python
import math

import jax
import jax.numpy as jnp
from jax import lax
from jax.experimental import pallas as pl
from jax.experimental.pallas import tpu as pltpu
from jax.sharding import PartitionSpec as P

MESH = pl.DeviceIdType.MESH
HEADS = 64
KVH = 8
HEAD_DIM = 128
ROWS = 128
N_DC = 64
N_TP = 8
PER = HEADS // KVH
REACH = 32
SLOTS = 34
PAIR = 2 * ROWS
CAP = 4
GROUP = 4
TILE = CAP * GROUP
DEAD = -1e30
V0, K0, D0, Z0, END = 0, 128, 256, 272, 384
SCALE = math.log2(math.e) / math.sqrt(HEAD_DIM)
F32, BF16, I32 = jnp.float32, jnp.bfloat16, jnp.int32


def iota(shape, dim):
    return lax.broadcasted_iota(I32, shape, dim)


def kernel(
    q_hbm, k_hbm, v_hbm, doc_ref, own_ref, out_ref,
    kin, qin, slots, neg, scores, peak, pack, unpack, context, packed, got, owners,
    kv_send, kv_recv, q_send, q_recv, own_send, own_recv, spread_send, spread_recv, out_send, out_recv,
):
    me = lax.axis_index("dc")
    tp = lax.axis_index("tp")

    barrier = pltpu.get_barrier_semaphore()

    @pl.loop(1, N_TP)
    def _(j):
        pl.semaphore_signal(barrier, inc=1, device_id=(me, lax.rem(tp + j, N_TP)), device_id_type=MESH)

    @pl.loop(1, N_DC)
    def _(j):
        pl.semaphore_signal(barrier, inc=1, device_id=(lax.rem(me + j, N_DC), tp), device_id_type=MESH)

    pl.semaphore_wait(barrier, N_TP - 1 + N_DC - 1)

    mine = pl.ds(pl.multiple_of(tp * 16, 16), 16)

    def columns(t, width):
        return pl.ds(pl.multiple_of(t * width, width), width)

    def part(source, t, width, target, send, recv):
        return pltpu.make_async_remote_copy(
            src_ref=source.at[:, columns(t, width)], dst_ref=target, send_sem=send, recv_sem=recv,
            device_id=(me, t), device_id_type=MESH,
        )

    value_target = slots.at[0, pl.ds(pl.multiple_of(V0 + tp * 16, 16), 16), :]

    @pl.loop(1, N_TP)
    def _(j):
        t = lax.rem(tp + j, N_TP)
        part(k_hbm, t, HEAD_DIM, kin.at[mine, :], kv_send.at[0], kv_recv.at[0]).start()
        part(v_hbm, t, HEAD_DIM, value_target, kv_send.at[1], kv_recv.at[1]).start()

    pltpu.make_async_copy(k_hbm.at[:, columns(tp, HEAD_DIM)], kin.at[mine, :], kv_recv.at[0]).start()
    pltpu.make_async_copy(v_hbm.at[:, columns(tp, HEAD_DIM)], value_target, kv_recv.at[1]).start()

    @pl.loop(1, N_TP)
    def _(j):
        t = lax.rem(tp + j, N_TP)
        part(q_hbm, t, PER * HEAD_DIM, qin.at[mine, :], q_send, q_recv).start()

    pltpu.make_async_copy(q_hbm.at[:, columns(tp, PER * HEAD_DIM)], qin.at[mine, :], q_recv).start()

    @pl.loop(1, N_DC)
    def _(j):
        pltpu.make_async_remote_copy(
            src_ref=own_ref, dst_ref=owners.at[me], send_sem=own_send, recv_sem=own_recv,
            device_id=(lax.rem(me + j, N_DC), tp), device_id_type=MESH,
        ).start()

    pltpu.make_async_copy(own_ref, owners.at[me], own_recv).start()

    slots[:, Z0:END, :] = jnp.zeros((SLOTS, END - Z0, ROWS), BF16)
    reach = jnp.minimum(me, REACH)

    @pl.loop(reach + 1, SLOTS)
    def _(r):
        slots[r, V0:D0, :] = jnp.zeros((D0 - V0, ROWS), BF16)
        slots[r, D0:Z0, :] = jnp.ones((Z0 - D0, ROWS), BF16)

    doc = doc_ref[...]
    slots[0, D0:Z0, :] = jnp.where(iota((Z0 - D0, ROWS), 0) == doc, 1.0, 0.0).astype(BF16)
    other = jnp.where((iota((ROWS, ROWS), 0) != doc) & (iota((ROWS, ROWS), 0) < Z0 - D0), DEAD, 0.0)
    neg[...] = other.T.astype(BF16)

    owner = own_ref[...]
    owner_col = jnp.broadcast_to(owner, (ROWS, ROWS)).astype(F32).T
    same = (owner_col == owner.astype(F32)) & (iota((ROWS, ROWS), 0) < iota((ROWS, ROWS), 1))
    rank = jnp.sum(jnp.where(same, 1.0, 0.0), axis=0, keepdims=True).astype(I32)
    place = owner * TILE + rank
    target = jnp.concatenate([place + h * CAP for h in range(GROUP)], axis=1)

    @pl.loop(0, N_DC * TILE, step=128)
    def _(base):
        base = pl.multiple_of(base, 128)
        rows = iota((128, GROUP * ROWS), 0) + base
        pack[pl.ds(base, 128), :] = jnp.where(rows == target, 1.0, 0.0).astype(BF16)

    pltpu.make_async_copy(kin, kin, kv_recv.at[0]).wait()
    pltpu.make_async_copy(kin, kin, kv_recv.at[1]).wait()
    slots[0, K0:D0, :] = kin[...].astype(F32).T.astype(BF16)

    last = jnp.minimum(N_DC - 1 - me, REACH)

    def spread(r):
        return pltpu.make_async_remote_copy(
            src_ref=slots.at[0, pl.ds(0, Z0), :], dst_ref=slots.at[r, pl.ds(0, Z0), :],
            send_sem=spread_send.at[r], recv_sem=spread_recv.at[r],
            device_id=(me + r, tp), device_id_type=MESH,
        )

    @pl.loop(1, last + 1)
    def _(r):
        spread(r).start()

    pltpu.make_async_copy(owners, owners, own_recv).wait()
    hits = jnp.where(owners[...].reshape(N_DC, ROWS) == me, 1.0, 0.0).astype(BF16)
    counts = lax.dot_general(
        jnp.ones((8, ROWS), BF16), hits, (((1,), (1,)), ((), ())), preferred_element_type=F32
    ).astype(BF16)
    lane_source = iota((N_DC, N_DC * TILE), 1) // TILE
    row_source = iota((N_DC, N_DC * TILE), 0)
    count = jnp.dot(counts, jnp.where(lane_source == row_source, 1.0, 0.0).astype(BF16), preferred_element_type=F32)
    before = jnp.dot(counts, jnp.where(row_source < lane_source, 1.0, 0.0).astype(BF16), preferred_element_type=F32)
    lane = iota((1, N_DC * TILE), 1)
    turn = lane % CAP
    goal = jnp.where(
        turn < count[0:1].astype(I32), before[0:1].astype(I32) + turn + (lane // CAP % GROUP) * ROWS, -1
    )

    @pl.loop(0, GROUP * ROWS, step=64)
    def _(base):
        base = pl.multiple_of(base, 64)
        rows = iota((64, N_DC * TILE), 0) + base
        unpack[pl.ds(base, 64), :] = jnp.where(rows == goal, 1.0, 0.0).astype(BF16)

    pltpu.make_async_copy(qin, qin, q_recv).wait()

    def arrive(r):
        @pl.when((r >= 1) & (r <= reach))
        def _():
            here = slots.at[r, pl.ds(0, Z0), :]
            pltpu.make_async_copy(here, here, spread_recv.at[r]).wait()

    def key_pair(c):
        return jnp.concatenate([slots[2 * c, K0:END, :], slots[2 * c + 1, K0:END, :]], axis=1)

    def score(h, keys):
        queries = jnp.concatenate([qin[:, h * HEAD_DIM : (h + 1) * HEAD_DIM], neg[...]], axis=1)
        return jnp.dot(queries, keys, preferred_element_type=F32)

    arrive(1)
    keys = key_pair(0)
    live = iota((ROWS, PAIR), 1) <= jnp.where(iota((ROWS, PAIR), 1) < ROWS, iota((ROWS, PAIR), 0), PAIR)
    for h in range(PER):
        s = jnp.where(live, score(h, keys), DEAD)
        scores[h, 0] = s
        peak[h] = jnp.maximum(s[:, :ROWS], s[:, ROWS:])

    @pl.loop(1, SLOTS // 2)
    def _(c):
        arrive(2 * c)
        arrive(2 * c + 1)
        keys = key_pair(c)
        for h in range(PER):
            s = score(h, keys)
            scores[h, c] = s
            peak[h] = jnp.maximum(peak[h], jnp.maximum(s[:, :ROWS], s[:, ROWS:]))

    for g in range(PER // GROUP):

        @pl.loop(0, GROUP)
        def _(i):
            h = g * GROUP + i
            top = jnp.broadcast_to(jnp.max(peak[h], axis=1, keepdims=True), (ROWS, PAIR))
            total = jnp.zeros((ROWS, ROWS), F32)
            summed = jnp.zeros((ROWS, HEAD_DIM), F32)
            for c in range(SLOTS // 2):
                weights = jnp.exp2((scores[h, c] - top) * SCALE)
                total = total + (weights[:, :ROWS] + weights[:, ROWS:])
                values = jnp.concatenate([slots[2 * c, V0:K0, :], slots[2 * c + 1, V0:K0, :]], axis=0)
                summed = summed + jnp.dot(weights.astype(BF16), values, preferred_element_type=F32)
            result = summed / jnp.sum(total, axis=1, keepdims=True)
            context[pl.ds(pl.multiple_of(i * ROWS, ROWS), ROWS), :] = result.astype(BF16)

        packed[g] = jnp.dot(pack[...], context[...], preferred_element_type=F32).astype(BF16)

        def tile(r):
            return pl.ds(pl.multiple_of(r * TILE, TILE), TILE)

        @pl.loop(1, N_DC)
        def _(j):
            to = lax.rem(me + j, N_DC)
            pltpu.make_async_remote_copy(
                src_ref=packed.at[g, tile(to), :], dst_ref=got.at[g, tile(me), :],
                send_sem=out_send.at[g], recv_sem=out_recv.at[g], device_id=(to, tp), device_id_type=MESH,
            ).start()

        pltpu.make_async_copy(packed.at[g, tile(me), :], got.at[g, tile(me), :], out_recv.at[g]).start()

    for g in range(PER // GROUP):
        pltpu.make_async_copy(got.at[g], got.at[g], out_recv.at[g]).wait()
        rows = jnp.dot(unpack[...], got[g], preferred_element_type=F32).astype(BF16)
        for i in range(GROUP):
            h = g * GROUP + i
            out_ref[:, h * HEAD_DIM : (h + 1) * HEAD_DIM] = rows[i * ROWS : (i + 1) * ROWS]

    seven = kin.at[pl.ds(0, ROWS - 16), :]
    pltpu.make_async_copy(seven, seven, kv_send.at[0]).wait()
    pltpu.make_async_copy(seven, seven, kv_send.at[1]).wait()
    sent = qin.at[pl.ds(0, ROWS - 16), :]
    pltpu.make_async_copy(sent, sent, q_send).wait()
    sent = owners.at[pl.ds(0, N_DC - 1)]
    pltpu.make_async_copy(sent, sent, own_send).wait()

    @pl.loop(1, last + 1)
    def _(r):
        spread(r).wait_send()

    for g in range(PER // GROUP):
        sent = packed.at[g, pl.ds(0, (N_DC - 1) * TILE), :]
        pltpu.make_async_copy(sent, sent, out_send.at[g]).wait()


def per_device(queries, keys, values, document_index, owner):
    hbm = pl.BlockSpec(memory_space=pl.ANY)
    vmem = pl.BlockSpec(memory_space=pltpu.VMEM)
    dma = pltpu.SemaphoreType.DMA
    groups = PER // GROUP
    return pl.pallas_call(
        kernel,
        out_shape=jax.ShapeDtypeStruct((ROWS, PER * HEAD_DIM), BF16),
        in_specs=[hbm, hbm, hbm, vmem, vmem],
        out_specs=vmem,
        scratch_shapes=[
            pltpu.VMEM((ROWS, HEAD_DIM), BF16),
            pltpu.VMEM((ROWS, PER * HEAD_DIM), BF16),
            pltpu.VMEM((SLOTS, END, ROWS), BF16),
            pltpu.VMEM((ROWS, ROWS), BF16),
            pltpu.VMEM((PER, SLOTS // 2, ROWS, PAIR), F32),
            pltpu.VMEM((PER, ROWS, ROWS), F32),
            pltpu.VMEM((N_DC * TILE, GROUP * ROWS), BF16),
            pltpu.VMEM((GROUP * ROWS, N_DC * TILE), BF16),
            pltpu.VMEM((GROUP * ROWS, HEAD_DIM), BF16),
            pltpu.VMEM((groups, N_DC * TILE, HEAD_DIM), BF16),
            pltpu.VMEM((groups, N_DC * TILE, HEAD_DIM), BF16),
            pltpu.VMEM((N_DC, 1, ROWS), I32),
            dma((2,)), dma((2,)), dma, dma, dma, dma, dma((SLOTS,)), dma((SLOTS,)), dma((groups,)), dma((groups,)),
        ],
        compiler_params=pltpu.CompilerParams(
            collective_id=0, has_side_effects=True, vmem_limit_bytes=48 * 1024 * 1024
        ),
        cost_estimate=pl.CostEstimate(flops=2_300_000_000, bytes_accessed=4_000_000, transcendentals=4_500_000),
    )(queries, keys, values, document_index.reshape(1, ROWS), owner.reshape(1, ROWS))


def solution(mesh):
    return jax.shard_map(
        per_device,
        mesh=mesh,
        in_specs=(
            P(("dc", "tp"), None),
            P(("dc", "tp"), None),
            P(("dc", "tp"), None),
            P("dc"),
            P("dc"),
        ),
        out_specs=P("dc", "tp"),
        check_vma=False,
    )
```

```python
import math

import jax
import jax.numpy as jnp
from jax import lax
from jax.experimental import pallas as pl
from jax.experimental.pallas import tpu as pltpu
from jax.sharding import PartitionSpec as P

MESH = pl.DeviceIdType.MESH
HEADS = 64
KVH = 8
HEAD_DIM = 128
ROWS = 128
N_DC = 64
N_TP = 8
ROWS_OF_CHIPS, COLS = 8, 4
PER = HEADS // KVH
REACH = 32
SLOTS = 34
PAIR = 2 * ROWS
CAP = 4
GROUP = 4
TILE = CAP * GROUP
DEAD = -1e30
V0, K0, D0, Z0, END = 0, 128, 256, 272, 384
SCALE = math.log2(math.e) / math.sqrt(HEAD_DIM)
F32, BF16, I32 = jnp.float32, jnp.bfloat16, jnp.int32


def iota(shape, dim):
    return lax.broadcasted_iota(I32, shape, dim)


def kernel(
    q_hbm, k_hbm, v_hbm, doc_hbm, own_hbm, out_ref,
    kin, qin, slots, neg, scores, peak, pack, unpack, context, packed, got, owners, doc_ref, own_ref,
    kv_send, kv_recv, q_send, q_recv, own_send, own_recv, doc_sem, down_send, along_send, across_send, spread_recv, out_send, out_recv,
):
    me = lax.axis_index("dc")
    tp = lax.axis_index("tp")

    pltpu.make_async_copy(doc_hbm, doc_ref, doc_sem.at[0]).start()
    pltpu.make_async_copy(own_hbm, own_ref, doc_sem.at[1]).start()
    barrier = pltpu.get_barrier_semaphore()

    @pl.loop(1, N_TP)
    def _(j):
        pl.semaphore_signal(barrier, inc=1, device_id=(me, lax.rem(tp + j, N_TP)), device_id_type=MESH)

    @pl.loop(1, N_DC)
    def _(j):
        pl.semaphore_signal(barrier, inc=1, device_id=(lax.rem(me + j, N_DC), tp), device_id_type=MESH)

    pl.semaphore_wait(barrier, N_TP - 1 + N_DC - 1)

    mine = pl.ds(pl.multiple_of(tp * 16, 16), 16)

    def columns(t, width):
        return pl.ds(pl.multiple_of(t * width, width), width)

    def part(source, t, width, target, send, recv):
        return pltpu.make_async_remote_copy(
            src_ref=source.at[:, columns(t, width)], dst_ref=target, send_sem=send, recv_sem=recv,
            device_id=(me, t), device_id_type=MESH,
        )

    value_target = slots.at[0, pl.ds(pl.multiple_of(V0 + tp * 16, 16), 16), :]

    @pl.loop(1, N_TP)
    def _(j):
        t = lax.rem(tp + j, N_TP)
        part(k_hbm, t, HEAD_DIM, kin.at[mine, :], kv_send.at[0], kv_recv.at[0]).start()
        part(v_hbm, t, HEAD_DIM, value_target, kv_send.at[1], kv_recv.at[1]).start()

    pltpu.make_async_copy(k_hbm.at[:, columns(tp, HEAD_DIM)], kin.at[mine, :], kv_recv.at[0]).start()
    pltpu.make_async_copy(v_hbm.at[:, columns(tp, HEAD_DIM)], value_target, kv_recv.at[1]).start()

    @pl.loop(1, N_TP)
    def _(j):
        t = lax.rem(tp + j, N_TP)
        part(q_hbm, t, PER * HEAD_DIM, qin.at[mine, :], q_send, q_recv).start()

    pltpu.make_async_copy(q_hbm.at[:, columns(tp, PER * HEAD_DIM)], qin.at[mine, :], q_recv).start()

    pltpu.make_async_copy(own_hbm, own_ref, doc_sem.at[1]).wait()

    @pl.loop(1, N_DC)
    def _(j):
        pltpu.make_async_remote_copy(
            src_ref=own_ref, dst_ref=owners.at[me], send_sem=own_send, recv_sem=own_recv,
            device_id=(lax.rem(me + j, N_DC), tp), device_id_type=MESH,
        ).start()

    pltpu.make_async_copy(own_ref, owners.at[me], own_recv).start()

    slots[:, Z0:END, :] = jnp.zeros((SLOTS, END - Z0, ROWS), BF16)
    reach = jnp.minimum(me, REACH)

    @pl.loop(reach + 1, SLOTS)
    def _(r):
        slots[r, V0:D0, :] = jnp.zeros((D0 - V0, ROWS), BF16)
        slots[r, D0:Z0, :] = jnp.ones((Z0 - D0, ROWS), BF16)

    pltpu.make_async_copy(doc_hbm, doc_ref, doc_sem.at[0]).wait()
    doc = doc_ref[...]
    slots[0, D0:Z0, :] = jnp.where(iota((Z0 - D0, ROWS), 0) == doc, 1.0, 0.0).astype(BF16)
    other = jnp.where((iota((ROWS, ROWS), 0) != doc) & (iota((ROWS, ROWS), 0) < Z0 - D0), DEAD, 0.0)
    neg[...] = other.T.astype(BF16)

    owner = own_ref[...]
    owner_col = jnp.broadcast_to(owner, (ROWS, ROWS)).astype(F32).T
    same = (owner_col == owner.astype(F32)) & (iota((ROWS, ROWS), 0) < iota((ROWS, ROWS), 1))
    rank = jnp.sum(jnp.where(same, 1.0, 0.0), axis=0, keepdims=True).astype(I32)
    place = owner * TILE + rank
    target = jnp.concatenate([place + h * CAP for h in range(GROUP)], axis=1)

    @pl.loop(0, N_DC * TILE, step=128)
    def _(base):
        base = pl.multiple_of(base, 128)
        rows = iota((128, GROUP * ROWS), 0) + base
        pack[pl.ds(base, 128), :] = jnp.where(rows == target, 1.0, 0.0).astype(BF16)

    pltpu.make_async_copy(kin, kin, kv_recv.at[0]).wait()
    pltpu.make_async_copy(kin, kin, kv_recv.at[1]).wait()
    slots[0, K0:D0, :] = kin[...].astype(F32).T.astype(BF16)

    chip, core = me // 2, lax.rem(me, 2)
    row, col = chip // COLS, lax.rem(chip, COLS)

    def send(r, target, r_there, sem):
        return pltpu.make_async_remote_copy(
            src_ref=slots.at[r, pl.ds(0, Z0), :], dst_ref=slots.at[r_there, pl.ds(0, Z0), :],
            send_sem=sem, recv_sem=spread_recv.at[r_there], device_id=(target, tp), device_id_type=MESH,
        )

    def arrived(r):
        here = slots.at[r, pl.ds(0, Z0), :]
        pltpu.make_async_copy(here, here, spread_recv.at[r]).wait()

    def down(j):
        return (row >= j) & (row < ROWS_OF_CHIPS - 1), send(2 * COLS * j, me + 2 * COLS, 2 * COLS * (j + 1), down_send.at[j])

    def along(j, step):
        k = COLS * j + step
        return (row >= j) & (col + step >= 0) & (col + step < COLS), send(
            2 * COLS * j, me + 2 * step, 2 * k, along_send.at[j, step + COLS - 1]
        )

    def steps(j):
        return [s for s in range(1 - COLS, COLS) if s and 0 < COLS * j + s <= REACH // 2]

    def across(k):
        found = []
        if k < REACH // 2:
            found.append((core == 0, send(2 * k, me + 1, 2 * k + 1, across_send.at[k])))
        if k > 0:
            found.append((core == 1, send(2 * k, me - 1, 2 * k - 1, across_send.at[k])))
        return found

    def start(copies):
        for needed, copy in copies:
            pl.when(needed)(copy.start)

    def from_column(j):
        if j:
            pl.when(row >= j)(lambda: arrived(2 * COLS * j))
        if j < REACH // 2 // COLS:
            start([down(j)])
        start([along(j, s) for s in steps(j)])
        start([((row >= j) & core_ok, copy) for core_ok, copy in across(COLS * j)])

    def from_row(j):
        for s in steps(j):
            k = COLS * j + s

            @pl.when((row >= j) & (col - s >= 0) & (col - s < COLS))
            def _():
                arrived(2 * k)
                start(across(k))

    from_column(0)

    pltpu.make_async_copy(owners, owners, own_recv).wait()
    hits = jnp.where(owners[...].reshape(N_DC, ROWS) == me, 1.0, 0.0).astype(BF16)
    counts = lax.dot_general(
        jnp.ones((8, ROWS), BF16), hits, (((1,), (1,)), ((), ())), preferred_element_type=F32
    ).astype(BF16)
    lane_source = iota((N_DC, N_DC * TILE), 1) // TILE
    row_source = iota((N_DC, N_DC * TILE), 0)
    count = jnp.dot(counts, jnp.where(lane_source == row_source, 1.0, 0.0).astype(BF16), preferred_element_type=F32)
    before = jnp.dot(counts, jnp.where(row_source < lane_source, 1.0, 0.0).astype(BF16), preferred_element_type=F32)
    lane = iota((1, N_DC * TILE), 1)
    turn = lane % CAP
    goal = jnp.where(
        turn < count[0:1].astype(I32), before[0:1].astype(I32) + turn + (lane // CAP % GROUP) * ROWS, -1
    )

    @pl.loop(0, GROUP * ROWS, step=64)
    def _(base):
        base = pl.multiple_of(base, 64)
        rows = iota((64, N_DC * TILE), 0) + base
        unpack[pl.ds(base, 64), :] = jnp.where(rows == goal, 1.0, 0.0).astype(BF16)

    pltpu.make_async_copy(qin, qin, q_recv).wait()

    for j in range(1, REACH // 2 // COLS + 1):
        from_column(j)
        from_row(j - 1)
    from_row(REACH // 2 // COLS)

    def arrive(r):
        pl.when((lax.rem(r, 2) == 1) & (r <= reach))(lambda: arrived(r))

    def key_pair(c):
        return jnp.concatenate([slots[2 * c, K0:END, :], slots[2 * c + 1, K0:END, :]], axis=1)

    def score(h, keys):
        queries = jnp.concatenate([qin[:, h * HEAD_DIM : (h + 1) * HEAD_DIM], neg[...]], axis=1)
        return jnp.dot(queries, keys, preferred_element_type=F32)

    arrive(jnp.int32(1))
    keys = key_pair(0)
    live = iota((ROWS, PAIR), 1) <= jnp.where(iota((ROWS, PAIR), 1) < ROWS, iota((ROWS, PAIR), 0), PAIR)
    for h in range(PER):
        s = jnp.where(live, score(h, keys), DEAD)
        scores[h, 0] = s
        peak[h] = jnp.maximum(s[:, :ROWS], s[:, ROWS:])

    @pl.loop(1, SLOTS // 2)
    def _(c):
        arrive(2 * c)
        arrive(2 * c + 1)
        keys = key_pair(c)
        for h in range(PER):
            s = score(h, keys)
            scores[h, c] = s
            peak[h] = jnp.maximum(peak[h], jnp.maximum(s[:, :ROWS], s[:, ROWS:]))

    for g in range(PER // GROUP):

        @pl.loop(0, GROUP)
        def _(i):
            h = g * GROUP + i
            top = jnp.broadcast_to(jnp.max(peak[h], axis=1, keepdims=True), (ROWS, PAIR))
            total = jnp.zeros((ROWS, ROWS), F32)
            summed = jnp.zeros((ROWS, HEAD_DIM), F32)
            for c in range(SLOTS // 2):
                weights = jnp.exp2((scores[h, c] - top) * SCALE)
                total = total + (weights[:, :ROWS] + weights[:, ROWS:])
                values = jnp.concatenate([slots[2 * c, V0:K0, :], slots[2 * c + 1, V0:K0, :]], axis=0)
                summed = summed + jnp.dot(weights.astype(BF16), values, preferred_element_type=F32)
            result = summed / jnp.sum(total, axis=1, keepdims=True)
            context[pl.ds(pl.multiple_of(i * ROWS, ROWS), ROWS), :] = result.astype(BF16)

        packed[g] = jnp.dot(pack[...], context[...], preferred_element_type=F32).astype(BF16)

        def tile(r):
            return pl.ds(pl.multiple_of(r * TILE, TILE), TILE)

        @pl.loop(1, N_DC)
        def _(j):
            to = lax.rem(me + j, N_DC)
            pltpu.make_async_remote_copy(
                src_ref=packed.at[g, tile(to), :], dst_ref=got.at[g, tile(me), :],
                send_sem=out_send.at[g], recv_sem=out_recv.at[g], device_id=(to, tp), device_id_type=MESH,
            ).start()

        pltpu.make_async_copy(packed.at[g, tile(me), :], got.at[g, tile(me), :], out_recv.at[g]).start()

    for g in range(PER // GROUP):
        pltpu.make_async_copy(got.at[g], got.at[g], out_recv.at[g]).wait()
        rows = jnp.dot(unpack[...], got[g], preferred_element_type=F32).astype(BF16)
        for i in range(GROUP):
            h = g * GROUP + i
            out_ref[:, h * HEAD_DIM : (h + 1) * HEAD_DIM] = rows[i * ROWS : (i + 1) * ROWS]

    seven = kin.at[pl.ds(0, ROWS - 16), :]
    pltpu.make_async_copy(seven, seven, kv_send.at[0]).wait()
    pltpu.make_async_copy(seven, seven, kv_send.at[1]).wait()
    sent = qin.at[pl.ds(0, ROWS - 16), :]
    pltpu.make_async_copy(sent, sent, q_send).wait()
    sent = owners.at[pl.ds(0, N_DC - 1)]
    pltpu.make_async_copy(sent, sent, own_send).wait()

    def left(copies):
        for needed, copy in copies:
            pl.when(needed)(copy.wait_send)

    for j in range(REACH // 2 // COLS + 1):
        if j < REACH // 2 // COLS:
            left([down(j)])
        left([along(j, s) for s in steps(j)])

    @pl.loop(0, REACH // 2 + 1)
    def _(k):
        gone = slots.at[2 * k, pl.ds(0, Z0), :]
        passed = (k <= chip) & jnp.where(core == 0, k < REACH // 2, k > 0)
        pl.when(passed)(lambda: pltpu.make_async_copy(gone, gone, across_send.at[k]).wait())

    for g in range(PER // GROUP):
        sent = packed.at[g, pl.ds(0, (N_DC - 1) * TILE), :]
        pltpu.make_async_copy(sent, sent, out_send.at[g]).wait()


def per_device(queries, keys, values, document_index, owner):
    hbm = pl.BlockSpec(memory_space=pltpu.HBM)
    vmem = pl.BlockSpec(memory_space=pltpu.VMEM)
    dma = pltpu.SemaphoreType.DMA
    groups = PER // GROUP
    return pl.pallas_call(
        kernel,
        out_shape=jax.ShapeDtypeStruct((ROWS, PER * HEAD_DIM), BF16),
        in_specs=[hbm] * 5,
        out_specs=vmem,
        scratch_shapes=[
            pltpu.VMEM((ROWS, HEAD_DIM), BF16),
            pltpu.VMEM((ROWS, PER * HEAD_DIM), BF16),
            pltpu.VMEM((SLOTS, END, ROWS), BF16),
            pltpu.VMEM((ROWS, ROWS), BF16),
            pltpu.VMEM((PER, SLOTS // 2, ROWS, PAIR), F32),
            pltpu.VMEM((PER, ROWS, ROWS), F32),
            pltpu.VMEM((N_DC * TILE, GROUP * ROWS), BF16),
            pltpu.VMEM((GROUP * ROWS, N_DC * TILE), BF16),
            pltpu.VMEM((GROUP * ROWS, HEAD_DIM), BF16),
            pltpu.VMEM((groups, N_DC * TILE, HEAD_DIM), BF16),
            pltpu.VMEM((groups, N_DC * TILE, HEAD_DIM), BF16),
            pltpu.VMEM((N_DC, 1, ROWS), I32),
            pltpu.VMEM((1, ROWS), I32),
            pltpu.VMEM((1, ROWS), I32),
            dma((2,)), dma((2,)), dma, dma, dma, dma, dma((2,)),
            dma((4,)), dma((5, 7)), dma((REACH // 2 + 1,)), dma((SLOTS,)), dma((groups,)), dma((groups,)),
        ],
        compiler_params=pltpu.CompilerParams(
            collective_id=0, has_side_effects=True, vmem_limit_bytes=48 * 1024 * 1024
        ),
        cost_estimate=pl.CostEstimate(flops=2_300_000_000, bytes_accessed=4_000_000, transcendentals=4_500_000),
    )(queries, keys, values, document_index.reshape(1, ROWS), owner.reshape(1, ROWS))


def solution(mesh):
    return jax.shard_map(
        per_device,
        mesh=mesh,
        in_specs=(
            P(("dc", "tp"), None),
            P(("dc", "tp"), None),
            P(("dc", "tp"), None),
            P("dc"),
            P("dc"),
        ),
        out_specs=P("dc", "tp"),
        check_vma=False,
    )
```

```python
import functools
import math

import jax
import jax.numpy as jnp
from jax import lax
from jax.experimental import pallas as pl
from jax.experimental.pallas import tpu as pltpu
from jax.sharding import PartitionSpec as P

MESH = pl.DeviceIdType.MESH
HEADS = 64
KVH = 8
HEAD_DIM = 128
ROWS = 128
N_DC = 64
N_TP = 8
ROWS_OF_CHIPS, COLS = 8, 4
PER = HEADS // KVH
REACH = 32
SLOTS = 34
STEP = 8
CAP = 4
GROUP = 4
TILE = CAP * GROUP
DEAD = -1e30
V0, K0, D0, Z0, END = 0, 128, 256, 272, 384
PARTS = ((K0, Z0), (V0, K0))
VALUES = 1
SCALE = math.log2(math.e) / math.sqrt(HEAD_DIM)
F32, BF16, I32 = jnp.float32, jnp.bfloat16, jnp.int32


def iota(shape, dim):
    return lax.broadcasted_iota(I32, shape, dim)


def kernel(
    q_hbm, k_hbm, v_hbm, doc_hbm, own_hbm, out_ref,
    kin, qin, slots, neg, queries, peak, totals, weighted, pack, unpack, packed, got, owners, doc_ref, own_ref,
    kv_send, kv_recv, q_send, q_recv, own_send, own_recv, doc_sem, down_send, along_send, across_send, spread_recv, out_send, out_recv, heard,
):
    me = lax.axis_index("dc")
    tp = lax.axis_index("tp")

    pltpu.make_async_copy(doc_hbm, doc_ref, doc_sem.at[0]).start()
    pltpu.make_async_copy(own_hbm, own_ref, doc_sem.at[1]).start()
    chip, core = me // 2, lax.rem(me, 2)
    row, col = chip // COLS, lax.rem(chip, COLS)
    sibling = me + 1 - 2 * core

    def rows_on(n):
        return lax.rem(row + n + ROWS_OF_CHIPS, ROWS_OF_CHIPS) * 2 * COLS + 2 * col + core

    def greet(semaphore, device):
        pl.semaphore_signal(semaphore, inc=1, device_id=device, device_id_type=MESH)

    barrier = pltpu.get_barrier_semaphore()

    @pl.loop(1, N_TP)
    def _(j):
        greet(barrier, (me, lax.rem(tp + j, N_TP)))

    greet(barrier, (sibling, tp))
    for n in range(1, COLS):
        greet(barrier, (row * 2 * COLS + 2 * lax.rem(col + n, COLS) + core, tp))
    for n in (-1, 1):
        greet(barrier, (rows_on(n), tp))
    pl.semaphore_wait(barrier, N_TP - 1 + 1 + COLS - 1 + 2)

    def tell(stage):
        if stage == 0:
            greet(heard.at[0], (sibling, tp))
        elif stage == 3:
            greet(heard.at[3], (rows_on(4), tp))
        else:
            greet(heard.at[stage], (rows_on(stage), tp))
            greet(heard.at[stage], (rows_on(-stage), tp))

    def hear(stage):
        pl.semaphore_wait(heard.at[stage], 2 if stage in (1, 2) else 1)

    tell(0)

    mine = pl.ds(pl.multiple_of(tp * 16, 16), 16)

    def columns(t, width):
        return pl.ds(pl.multiple_of(t * width, width), width)

    def part(source, t, width, target, send, recv):
        return pltpu.make_async_remote_copy(
            src_ref=source.at[:, columns(t, width)], dst_ref=target, send_sem=send, recv_sem=recv,
            device_id=(me, t), device_id_type=MESH,
        )

    value_target = slots.at[0, pl.ds(pl.multiple_of(V0 + tp * 16, 16), 16), :]

    @pl.loop(1, N_TP)
    def _(j):
        t = lax.rem(tp + j, N_TP)
        part(k_hbm, t, HEAD_DIM, kin.at[mine, :], kv_send.at[0], kv_recv.at[0]).start()
        part(v_hbm, t, HEAD_DIM, value_target, kv_send.at[1], kv_recv.at[1]).start()

    pltpu.make_async_copy(k_hbm.at[:, columns(tp, HEAD_DIM)], kin.at[mine, :], kv_recv.at[0]).start()
    pltpu.make_async_copy(v_hbm.at[:, columns(tp, HEAD_DIM)], value_target, kv_recv.at[1]).start()

    @pl.loop(1, N_TP)
    def _(j):
        t = lax.rem(tp + j, N_TP)
        part(q_hbm, t, PER * HEAD_DIM, qin.at[mine, :], q_send, q_recv).start()

    pltpu.make_async_copy(q_hbm.at[:, columns(tp, PER * HEAD_DIM)], qin.at[mine, :], q_recv).start()

    slots[:, Z0:END, :] = jnp.zeros((SLOTS, END - Z0, ROWS), BF16)
    reach = jnp.minimum(me, REACH)

    @pl.loop(reach + 1, jnp.minimum((reach // STEP + 1) * STEP, SLOTS))
    def _(r):
        slots[r, V0:D0, :] = jnp.zeros((D0 - V0, ROWS), BF16)
        slots[r, D0:Z0, :] = jnp.ones((Z0 - D0, ROWS), BF16)

    pltpu.make_async_copy(doc_hbm, doc_ref, doc_sem.at[0]).wait()
    doc = doc_ref[...]
    slots[0, D0:Z0, :] = jnp.where(iota((Z0 - D0, ROWS), 0) == doc, 1.0, 0.0).astype(BF16)
    other = jnp.where((iota((ROWS, ROWS), 0) != doc) & (iota((ROWS, ROWS), 0) < Z0 - D0), DEAD, 0.0)
    neg[...] = other.T.astype(BF16)

    pltpu.make_async_copy(own_hbm, own_ref, doc_sem.at[1]).wait()
    owner = own_ref[...]
    owner_col = jnp.broadcast_to(owner, (ROWS, ROWS)).astype(F32).T
    same = (owner_col == owner.astype(F32)) & (iota((ROWS, ROWS), 0) < iota((ROWS, ROWS), 1))
    rank = jnp.sum(jnp.where(same, 1.0, 0.0), axis=0, keepdims=True).astype(I32)
    place = owner * TILE + rank
    target = jnp.concatenate([place + h * CAP for h in range(GROUP)], axis=1)

    @pl.loop(0, N_DC * TILE, step=128)
    def _(base):
        base = pl.multiple_of(base, 128)
        rows = iota((128, GROUP * ROWS), 0) + base
        pack[pl.ds(base, 128), :] = jnp.where(rows == target, 1.0, 0.0).astype(BF16)

    hear(0)
    tell(1)

    pltpu.make_async_copy(kin, kin, kv_recv.at[0]).wait()
    slots[0, K0:D0, :] = kin[...].astype(F32).T.astype(BF16)

    def rows_of(r, p):
        return slots.at[r, pl.ds(PARTS[p][0], PARTS[p][1] - PARTS[p][0]), :]

    def send(r, target, r_there, sem, p):
        return pltpu.make_async_remote_copy(
            src_ref=rows_of(r, p), dst_ref=rows_of(r_there, p), send_sem=sem.at[p],
            recv_sem=spread_recv.at[r_there, p], device_id=(target, tp), device_id_type=MESH,
        )

    def arrived(r, p):
        pltpu.make_async_copy(rows_of(r, p), rows_of(r, p), spread_recv.at[r, p]).wait()

    def down(j, p):
        there = 2 * COLS * (j + 1)
        return (row >= j) & (row < ROWS_OF_CHIPS - 1), send(2 * COLS * j, me + 2 * COLS, there, down_send.at[j], p)

    def along(j, step, p):
        k = COLS * j + step
        return (row >= j) & (col + step >= 0) & (col + step < COLS), send(
            2 * COLS * j, me + 2 * step, 2 * k, along_send.at[j, step + COLS - 1], p
        )

    def steps(j):
        return [s for s in range(1 - COLS, COLS) if s and 0 < COLS * j + s <= REACH // 2]

    def across(k, p):
        found = []
        if k < REACH // 2:
            found.append((core == 0, send(2 * k, me + 1, 2 * k + 1, across_send.at[k], p)))
        if k > 0:
            found.append((core == 1, send(2 * k, me - 1, 2 * k - 1, across_send.at[k], p)))
        return found

    def start(copies):
        for needed, copy in copies:
            pl.when(needed)(copy.start)

    def from_column(j):
        for p in range(len(PARTS)):
            if j:
                pl.when(row >= j)(functools.partial(arrived, 2 * COLS * j, p))
            elif p == VALUES:
                pltpu.make_async_copy(kin, kin, kv_recv.at[1]).wait()
            if j < REACH // 2 // COLS:
                start([down(j, p)])
            start([along(j, s, p) for s in steps(j)])
            start([((row >= j) & its_core, copy) for its_core, copy in across(COLS * j, p)])

    def from_row(j):
        for p in range(len(PARTS)):
            for s in steps(j):
                k = COLS * j + s

                @pl.when((row >= j) & (col - s >= 0) & (col - s < COLS))
                def _():
                    arrived(2 * k, p)
                    start(across(k, p))

    from_column(0)

    def arrive(r):
        @pl.when((lax.rem(r, 2) == 1) & (r <= reach))
        def _():
            for p in range(len(PARTS)):
                arrived(r, p)

    def attend(step, group):
        base = step * STEP
        count = min(STEP, SLOTS - base)
        at = pl.ds(group * GROUP * ROWS, GROUP * ROWS)
        keys = jnp.concatenate([slots[base + i, K0:END, :] for i in range(count)], axis=1)
        values = jnp.concatenate([slots[base + i, V0:K0, :] for i in range(count)], axis=0)
        s = jnp.dot(queries[at, :], keys, preferred_element_type=F32)
        s = [s[:, i * ROWS : (i + 1) * ROWS] for i in range(count)]
        if step == 0:
            row_of = lax.rem(iota((GROUP * ROWS, ROWS), 0), ROWS)
            s[0] = jnp.where(iota((GROUP * ROWS, ROWS), 1) <= row_of, s[0], DEAD)
        top = jnp.max(functools.reduce(jnp.maximum, s), axis=1, keepdims=True)
        if step == 0:
            top = jnp.broadcast_to(top, (GROUP * ROWS, ROWS))
        else:
            old = peak[at, :]
            top = jnp.maximum(old, top)
            shrink = jnp.exp2((old - top) * SCALE)
        weights = [jnp.exp2((x - top) * SCALE) for x in s]
        total = functools.reduce(jnp.add, weights)
        rounded = jnp.concatenate([w.astype(BF16) for w in weights], axis=1)
        summed = jnp.dot(rounded, values, preferred_element_type=F32)
        if step > 0:
            total = totals[at, :] * shrink + total
            summed = weighted[at, :] * shrink + summed
        peak[at, :] = top
        totals[at, :] = total
        weighted[at, :] = summed

    def step_of(step, groups):
        def run():
            for i in range(1, min(STEP, SLOTS - step * STEP), 2):
                if groups[0] == 0:
                    arrive(jnp.int32(step * STEP + i))
            for g in groups:
                attend(step, g)

        if step:
            pl.when(reach >= step * STEP)(run)
        else:
            run()

    every = tuple(range(PER // GROUP))
    from_column(1)
    hear(1)
    tell(2)
    from_row(0)
    from_column(2)
    hear(2)
    tell(3)
    from_row(1)
    from_column(3)
    from_row(2)
    hear(3)

    @pl.loop(1, N_DC)
    def _(j):
        pltpu.make_async_remote_copy(
            src_ref=own_ref, dst_ref=owners.at[me], send_sem=own_send, recv_sem=own_recv,
            device_id=(lax.rem(me + j, N_DC), tp), device_id_type=MESH,
        ).start()

    pltpu.make_async_copy(own_ref, owners.at[me], own_recv).start()

    pltpu.make_async_copy(qin, qin, q_recv).wait()
    for h in range(PER):
        queries[h * ROWS : (h + 1) * ROWS, :HEAD_DIM] = qin[:, h * HEAD_DIM : (h + 1) * HEAD_DIM]
        queries[h * ROWS : (h + 1) * ROWS, HEAD_DIM:] = neg[...]
    step_of(0, every)
    from_column(4)
    from_row(3)
    step_of(1, every)
    from_row(4)
    step_of(2, every)

    for g in every:
        step_of(3, (g,))
        step_of(4, (g,))
        at = pl.ds(g * GROUP * ROWS, GROUP * ROWS)
        context = (weighted[at, :] / jnp.sum(totals[at, :], axis=1, keepdims=True)).astype(BF16)
        packed[g] = jnp.dot(pack[...], context, preferred_element_type=F32).astype(BF16)

        def tile(r):
            return pl.ds(pl.multiple_of(r * TILE, TILE), TILE)

        @pl.loop(1, N_DC)
        def _(j):
            to = lax.rem(me + j, N_DC)
            pltpu.make_async_remote_copy(
                src_ref=packed.at[g, tile(to), :], dst_ref=got.at[g, tile(me), :],
                send_sem=out_send.at[g], recv_sem=out_recv.at[g], device_id=(to, tp), device_id_type=MESH,
            ).start()

        pltpu.make_async_copy(packed.at[g, tile(me), :], got.at[g, tile(me), :], out_recv.at[g]).start()

    pltpu.make_async_copy(owners, owners, own_recv).wait()
    hits = jnp.where(owners[...].reshape(N_DC, ROWS) == me, 1.0, 0.0).astype(BF16)
    counts = lax.dot_general(
        jnp.ones((8, ROWS), BF16), hits, (((1,), (1,)), ((), ())), preferred_element_type=F32
    ).astype(BF16)
    lane_source = iota((N_DC, N_DC * TILE), 1) // TILE
    row_source = iota((N_DC, N_DC * TILE), 0)
    count = jnp.dot(counts, jnp.where(lane_source == row_source, 1.0, 0.0).astype(BF16), preferred_element_type=F32)
    before = jnp.dot(counts, jnp.where(row_source < lane_source, 1.0, 0.0).astype(BF16), preferred_element_type=F32)
    lane = iota((1, N_DC * TILE), 1)
    turn = lane % CAP
    goal = jnp.where(
        turn < count[0:1].astype(I32), before[0:1].astype(I32) + turn + (lane // CAP % GROUP) * ROWS, -1
    )

    @pl.loop(0, GROUP * ROWS, step=64)
    def _(base):
        base = pl.multiple_of(base, 64)
        rows = iota((64, N_DC * TILE), 0) + base
        unpack[pl.ds(base, 64), :] = jnp.where(rows == goal, 1.0, 0.0).astype(BF16)

    for g in range(PER // GROUP):
        pltpu.make_async_copy(got.at[g], got.at[g], out_recv.at[g]).wait()
        rows = jnp.dot(unpack[...], got[g], preferred_element_type=F32).astype(BF16)
        for i in range(GROUP):
            h = g * GROUP + i
            out_ref[:, h * HEAD_DIM : (h + 1) * HEAD_DIM] = rows[i * ROWS : (i + 1) * ROWS]

    seven = kin.at[pl.ds(0, ROWS - 16), :]
    pltpu.make_async_copy(seven, seven, kv_send.at[0]).wait()
    pltpu.make_async_copy(seven, seven, kv_send.at[1]).wait()
    sent = qin.at[pl.ds(0, ROWS - 16), :]
    pltpu.make_async_copy(sent, sent, q_send).wait()
    sent = owners.at[pl.ds(0, N_DC - 1)]
    pltpu.make_async_copy(sent, sent, own_send).wait()

    def left(copies):
        for needed, copy in copies:
            pl.when(needed)(copy.wait_send)

    for p in range(len(PARTS)):
        for j in range(REACH // 2 // COLS + 1):
            if j < REACH // 2 // COLS:
                left([down(j, p)])
            left([along(j, s, p) for s in steps(j)])

        @pl.loop(0, REACH // 2 + 1)
        def _(k):
            gone = rows_of(2 * k, p)
            passed = (k <= chip) & jnp.where(core == 0, k < REACH // 2, k > 0)
            pl.when(passed)(lambda: pltpu.make_async_copy(gone, gone, across_send.at[k, p]).wait())

    for g in range(PER // GROUP):
        sent = packed.at[g, pl.ds(0, (N_DC - 1) * TILE), :]
        pltpu.make_async_copy(sent, sent, out_send.at[g]).wait()


def per_device(queries, keys, values, document_index, owner):
    hbm = pl.BlockSpec(memory_space=pltpu.HBM)
    vmem = pl.BlockSpec(memory_space=pltpu.VMEM)
    dma = pltpu.SemaphoreType.DMA
    groups, parts = PER // GROUP, len(PARTS)
    return pl.pallas_call(
        kernel,
        out_shape=jax.ShapeDtypeStruct((ROWS, PER * HEAD_DIM), BF16),
        in_specs=[hbm] * 5,
        out_specs=vmem,
        scratch_shapes=[
            pltpu.VMEM((ROWS, HEAD_DIM), BF16),
            pltpu.VMEM((ROWS, PER * HEAD_DIM), BF16),
            pltpu.VMEM((SLOTS, END, ROWS), BF16),
            pltpu.VMEM((ROWS, ROWS), BF16),
            pltpu.VMEM((PER * ROWS, 2 * HEAD_DIM), BF16),
            pltpu.VMEM((PER * ROWS, ROWS), F32),
            pltpu.VMEM((PER * ROWS, ROWS), F32),
            pltpu.VMEM((PER * ROWS, HEAD_DIM), F32),
            pltpu.VMEM((N_DC * TILE, GROUP * ROWS), BF16),
            pltpu.VMEM((GROUP * ROWS, N_DC * TILE), BF16),
            pltpu.VMEM((groups, N_DC * TILE, HEAD_DIM), BF16),
            pltpu.VMEM((groups, N_DC * TILE, HEAD_DIM), BF16),
            pltpu.VMEM((N_DC, 1, ROWS), I32),
            pltpu.VMEM((1, ROWS), I32),
            pltpu.VMEM((1, ROWS), I32),
            dma((2,)), dma((2,)), dma, dma, dma, dma, dma((2,)),
            dma((4, parts)), dma((5, 7, parts)), dma((REACH // 2 + 1, parts)), dma((SLOTS, parts)), dma((groups,)), dma((groups,)),
            pltpu.SemaphoreType.REGULAR((4,)),
        ],
        compiler_params=pltpu.CompilerParams(
            collective_id=0, has_side_effects=True, vmem_limit_bytes=63 * 1024 * 1024
        ),
        cost_estimate=pl.CostEstimate(flops=2_300_000_000, bytes_accessed=4_000_000, transcendentals=4_500_000),
    )(queries, keys, values, document_index.reshape(1, ROWS), owner.reshape(1, ROWS))


def solution(mesh):
    return jax.shard_map(
        per_device,
        mesh=mesh,
        in_specs=(
            P(("dc", "tp"), None),
            P(("dc", "tp"), None),
            P(("dc", "tp"), None),
            P("dc"),
            P("dc"),
        ),
        out_specs=P("dc", "tp"),
        check_vma=False,
    )
```

```python
import functools
import math

import jax
import jax.numpy as jnp
from jax import lax
from jax.experimental import pallas as pl
from jax.experimental.pallas import tpu as pltpu
from jax.sharding import PartitionSpec as P

MESH = pl.DeviceIdType.MESH
HEADS = 64
KVH = 8
HEAD_DIM = 128
ROWS = 128
N_DC = 64
N_TP = 8
ROWS_OF_CHIPS, COLS = 8, 4
CHIPS = ROWS_OF_CHIPS * COLS
PER = HEADS // KVH
REACH = 32
SLOTS = 34
STEP = 8
CAP = 4
GROUP = 4
TILE = CAP * GROUP
DEAD = -1e30
V0, K0, D0, Z0, END = 0, 128, 256, 272, 384
PARTS = ((K0, Z0), (V0, K0))
DOWN = {0: (1,), 1: (1,), 2: (1,), 3: (1,)}
VALUES = 1
SCALE = math.log2(math.e) / math.sqrt(HEAD_DIM)
F32, BF16, I32 = jnp.float32, jnp.bfloat16, jnp.int32


def iota(shape, dim):
    return lax.broadcasted_iota(I32, shape, dim)


def kernel(
    q_hbm, k_hbm, v_hbm, doc_hbm, own_hbm, out_ref,
    kin, qin, slots, neg, queries, peak, totals, weighted, pack, unpack, packed, landed, handed, attended, owners, places, doc_ref, own_ref,
    kv_send, kv_recv, q_send, q_recv, own_send, own_recv, place_send, place_recv, doc_sem, down_send, below_send, along_send, across_send, spread_recv, out_send, out_recv, hand_send, hand_recv, out_sem, heard,
):
    me = lax.axis_index("dc")
    tp = lax.axis_index("tp")

    pltpu.make_async_copy(doc_hbm, doc_ref, doc_sem.at[0]).start()
    pltpu.make_async_copy(own_hbm, own_ref, doc_sem.at[1]).start()
    chip, core = me // 2, lax.rem(me, 2)
    row, col = chip // COLS, lax.rem(chip, COLS)
    sibling = me + 1 - 2 * core

    def rows_on(n):
        return lax.rem(row + n + ROWS_OF_CHIPS, ROWS_OF_CHIPS) * 2 * COLS + 2 * col + core

    def greet(semaphore, device):
        pl.semaphore_signal(semaphore, inc=1, device_id=device, device_id_type=MESH)

    barrier = pltpu.get_barrier_semaphore()

    @pl.loop(1, N_TP)
    def _(j):
        greet(barrier, (me, lax.rem(tp + j, N_TP)))

    greet(barrier, (sibling, tp))
    for n in range(1, COLS):
        greet(barrier, (row * 2 * COLS + 2 * lax.rem(col + n, COLS) + core, tp))
    for n in (-1, 1):
        greet(barrier, (rows_on(n), tp))
    pl.semaphore_wait(barrier, N_TP - 1 + 1 + COLS - 1 + 2)

    def tell(stage):
        if stage == 2:
            greet(heard.at[2], (rows_on(4), tp))
        else:
            greet(heard.at[stage], (rows_on(stage + 1), tp))
            greet(heard.at[stage], (rows_on(-stage - 1), tp))

    def hear(stage):
        pl.semaphore_wait(heard.at[stage], 1 if stage == 2 else 2)

    tell(0)

    mine = pl.ds(pl.multiple_of(tp * 16, 16), 16)

    def columns(t, width):
        return pl.ds(pl.multiple_of(t * width, width), width)

    def part(source, t, width, target, send, recv):
        return pltpu.make_async_remote_copy(
            src_ref=source.at[:, columns(t, width)], dst_ref=target, send_sem=send, recv_sem=recv,
            device_id=(me, t), device_id_type=MESH,
        )

    value_target = slots.at[0, pl.ds(pl.multiple_of(V0 + tp * 16, 16), 16), :]

    @pl.loop(1, N_TP)
    def _(j):
        t = lax.rem(tp + j, N_TP)
        part(k_hbm, t, HEAD_DIM, kin.at[mine, :], kv_send.at[0], kv_recv.at[0]).start()
        part(v_hbm, t, HEAD_DIM, value_target, kv_send.at[1], kv_recv.at[1]).start()

    pltpu.make_async_copy(k_hbm.at[:, columns(tp, HEAD_DIM)], kin.at[mine, :], kv_recv.at[0]).start()
    pltpu.make_async_copy(v_hbm.at[:, columns(tp, HEAD_DIM)], value_target, kv_recv.at[1]).start()

    @pl.loop(1, N_TP)
    def _(j):
        t = lax.rem(tp + j, N_TP)
        part(q_hbm, t, PER * HEAD_DIM, qin.at[mine, :], q_send, q_recv).start()

    pltpu.make_async_copy(q_hbm.at[:, columns(tp, PER * HEAD_DIM)], qin.at[mine, :], q_recv).start()

    slots[:, Z0:END, :] = jnp.zeros((SLOTS, END - Z0, ROWS), BF16)
    reach = jnp.minimum(me, REACH)

    @pl.loop(reach + 1, jnp.minimum((reach // STEP + 1) * STEP, SLOTS))
    def _(r):
        slots[r, V0:D0, :] = jnp.zeros((D0 - V0, ROWS), BF16)
        slots[r, D0:Z0, :] = jnp.ones((Z0 - D0, ROWS), BF16)

    pltpu.make_async_copy(doc_hbm, doc_ref, doc_sem.at[0]).wait()
    doc = doc_ref[...]
    slots[0, D0:Z0, :] = jnp.where(iota((Z0 - D0, ROWS), 0) == doc, 1.0, 0.0).astype(BF16)
    other = jnp.where((iota((ROWS, ROWS), 0) != doc) & (iota((ROWS, ROWS), 0) < Z0 - D0), DEAD, 0.0)
    neg[...] = other.T.astype(BF16)

    pltpu.make_async_copy(own_hbm, own_ref, doc_sem.at[1]).wait()
    owner = own_ref[...]
    owner_col = jnp.broadcast_to(owner, (ROWS, ROWS)).astype(F32).T
    same = (owner_col == owner.astype(F32)) & (iota((ROWS, ROWS), 0) < iota((ROWS, ROWS), 1))
    rank = jnp.sum(jnp.where(same, 1.0, 0.0), axis=0, keepdims=True).astype(I32)
    place = owner * TILE + rank
    target = jnp.concatenate([place + h * CAP for h in range(GROUP)], axis=1)

    @pl.loop(0, N_DC * TILE, step=128)
    def _(base):
        base = pl.multiple_of(base, 128)
        rows = iota((128, GROUP * ROWS), 0) + base
        pack[pl.ds(base, 128), :] = jnp.where(rows == target, 1.0, 0.0).astype(BF16)

    hear(0)
    tell(1)

    pltpu.make_async_copy(kin, kin, kv_recv.at[0]).wait()
    slots[0, K0:D0, :] = kin[...].astype(F32).T.astype(BF16)

    def rows_of(r, p):
        return slots.at[r, pl.ds(PARTS[p][0], PARTS[p][1] - PARTS[p][0]), :]

    def send(r, target, r_there, sem, p):
        return pltpu.make_async_remote_copy(
            src_ref=rows_of(r, p), dst_ref=rows_of(r_there, p), send_sem=sem.at[p],
            recv_sem=spread_recv.at[r_there, p], device_id=(target, tp), device_id_type=MESH,
        )

    def arrived(r, p):
        pltpu.make_async_copy(rows_of(r, p), rows_of(r, p), spread_recv.at[r, p]).wait()

    def down(j, p):
        found = []
        for n in DOWN.get(j, ()):
            there = 2 * COLS * (j + n)
            copy = send(2 * COLS * j, me + 2 * COLS * n, there, down_send.at[j + n - 1], p)
            found.append(((row >= j) & (row + n < ROWS_OF_CHIPS), copy))
        return found

    def along(j, step, p):
        k = COLS * j + step
        return (row >= j) & (col + step >= 0) & (col + step < COLS), send(
            2 * COLS * j, me + 2 * step, 2 * k, along_send.at[j, step + COLS - 1], p
        )

    def steps(j):
        return [s for s in range(1 - COLS, COLS) if s and 0 < COLS * j + s <= REACH // 2]

    def sideways(j):
        return [s for s in steps(j) if abs(s) != 2 or j < 2]

    def below(j, p):
        found = []
        for s in (2, -2):
            k = COLS * j + s
            if j and k + COLS <= REACH // 2:
                copy = send(2 * k, me + 2 * COLS, 2 * (k + COLS), below_send.at[j], p)
                there = (row >= j) & (row < ROWS_OF_CHIPS - 1) & (col - s >= 0) & (col - s < COLS)
                found.append((there, copy))
        return found

    def across(k, p):
        found = []
        if k < REACH // 2:
            found.append((core == 0, send(2 * k, me + 1, 2 * k + 1, across_send.at[k], p)))
        if k > 0:
            found.append((core == 1, send(2 * k, me - 1, 2 * k - 1, across_send.at[k], p)))
        return found

    def start(copies):
        for needed, copy in copies:
            pl.when(needed)(copy.start)

    def from_column(j):
        for p in range(len(PARTS)):
            if j:
                pl.when(row >= j)(functools.partial(arrived, 2 * COLS * j, p))
            elif p == VALUES:
                pltpu.make_async_copy(kin, kin, kv_recv.at[1]).wait()
            start(down(j, p))
            start([along(j, s, p) for s in sideways(j)])
            start([((row >= j) & its_core, copy) for its_core, copy in across(COLS * j, p)])

    def from_row(j):
        for p in range(len(PARTS)):
            for s in sorted(steps(j), key=lambda s: abs(s) != 2):
                k = COLS * j + s

                @pl.when((row >= j) & (col - s >= 0) & (col - s < COLS))
                def _():
                    arrived(2 * k, p)
                    if abs(s) == 2:
                        start(below(j, p))
                    start(across(k, p))

    from_column(0)

    def send_owner():
        for i in range(COLS):
            there = tp * COLS + i
            pl.when(there != chip)(pltpu.make_async_remote_copy(
                src_ref=own_ref, dst_ref=owners.at[core, chip], send_sem=own_send.at[i], recv_sem=own_recv.at[0],
                device_id=(2 * there + core, tp), device_id_type=MESH,
            ).start)
        pl.when(row == tp)(pltpu.make_async_copy(own_ref, owners.at[core, chip], own_recv.at[0]).start)

    def swap_owners():
        return pltpu.make_async_remote_copy(
            src_ref=owners.at[core], dst_ref=owners.at[core], send_sem=own_send.at[COLS], recv_sem=own_recv.at[1],
            device_id=(sibling, tp), device_id_type=MESH,
        )

    def gather_owners():
        pltpu.make_async_copy(owners.at[core], owners.at[core], own_recv.at[0]).wait()
        swap_owners().start()

    def send_places():
        swap_owners().wait()
        hits = jnp.where(owners[...].reshape(N_DC, ROWS) == me, 1.0, 0.0).astype(BF16)
        counts = lax.dot_general(
            jnp.ones((8, ROWS), BF16), hits, (((1,), (1,)), ((), ())), preferred_element_type=F32
        ).astype(BF16)
        lane = iota((1, N_DC * TILE), 1)
        turn = lax.rem(lane, CAP)
        from_core = jnp.where(lane < N_DC * TILE // 2, core, 1 - core)
        source = 2 * lax.rem(lane // TILE, CHIPS) + from_core
        listed = iota((N_DC, N_DC * TILE), 0)
        listed = 2 * lax.rem(listed, CHIPS) + listed // CHIPS
        count = jnp.dot(counts, jnp.where(listed == source, 1.0, 0.0).astype(BF16), preferred_element_type=F32)
        before = jnp.dot(counts, jnp.where(listed < source, 1.0, 0.0).astype(BF16), preferred_element_type=F32)
        head = lax.rem(lane // CAP, GROUP)
        places[...] = jnp.where(turn < count[0:1].astype(I32), before[0:1].astype(I32) + turn + head * ROWS, -1)

        @pl.loop(1, N_TP)
        def _(j):
            pltpu.make_async_remote_copy(
                src_ref=places, dst_ref=places, send_sem=place_send.at[j], recv_sem=place_recv,
                device_id=(me, lax.rem(tp + j, N_TP)), device_id_type=MESH,
            ).start()

    def arrive(r):
        @pl.when((lax.rem(r, 2) == 1) & (r <= reach))
        def _():
            for p in range(len(PARTS)):
                arrived(r, p)

    def attend(step, group):
        base = step * STEP
        count = min(STEP, SLOTS - base)
        at = pl.ds(group * GROUP * ROWS, GROUP * ROWS)
        keys = jnp.concatenate([slots[base + i, K0:END, :] for i in range(count)], axis=1)
        values = jnp.concatenate([slots[base + i, V0:K0, :] for i in range(count)], axis=0)
        s = jnp.dot(queries[at, :], keys, preferred_element_type=F32)
        s = [s[:, i * ROWS : (i + 1) * ROWS] for i in range(count)]
        if step == 0:
            row_of = lax.rem(iota((GROUP * ROWS, ROWS), 0), ROWS)
            s[0] = jnp.where(iota((GROUP * ROWS, ROWS), 1) <= row_of, s[0], DEAD)
        top = jnp.max(functools.reduce(jnp.maximum, s), axis=1, keepdims=True)
        if step == 0:
            top = jnp.broadcast_to(top, (GROUP * ROWS, ROWS))
        else:
            old = peak[at, :]
            top = jnp.maximum(old, top)
            shrink = jnp.exp2((old - top) * SCALE)
        weights = [jnp.exp2((x - top) * SCALE) for x in s]
        total = functools.reduce(jnp.add, weights)
        rounded = jnp.concatenate([w.astype(BF16) for w in weights], axis=1)
        summed = jnp.dot(rounded, values, preferred_element_type=F32)
        if step > 0:
            total = totals[at, :] * shrink + total
            summed = weighted[at, :] * shrink + summed
        peak[at, :] = top
        totals[at, :] = total
        weighted[at, :] = summed

    def step_of(step, groups):
        def run():
            for i in range(1, min(STEP, SLOTS - step * STEP), 2):
                if groups[0] == 0:
                    arrive(jnp.int32(step * STEP + i))
            for g in groups:
                attend(step, g)

        if step:
            pl.when(reach >= step * STEP)(run)
        else:
            run()

    every = tuple(range(PER // GROUP))
    from_column(1)
    hear(1)
    tell(2)
    from_row(0)
    from_column(2)
    from_row(1)
    hear(2)
    send_owner()
    from_column(3)
    pltpu.make_async_copy(qin, qin, q_recv).wait()
    for h in range(PER):
        queries[h * ROWS : (h + 1) * ROWS, :HEAD_DIM] = qin[:, h * HEAD_DIM : (h + 1) * HEAD_DIM]
        queries[h * ROWS : (h + 1) * ROWS, HEAD_DIM:] = neg[...]
    step_of(0, (0,))
    from_row(2)
    step_of(0, (1,))
    from_column(4)
    step_of(1, (0,))
    from_row(3)
    pl.when(row == tp)(gather_owners)
    step_of(1, (1,))
    step_of(2, (0,))
    step_of(2, (1,))
    pl.when(row == tp)(send_places)
    from_row(4)

    for g in every:
        step_of(3, (g,))
        step_of(4, (g,))
        at = pl.ds(g * GROUP * ROWS, GROUP * ROWS)
        context = (weighted[at, :] / jnp.sum(totals[at, :], axis=1, keepdims=True)).astype(BF16)
        packed[g] = jnp.dot(pack[...], context, preferred_element_type=F32).astype(BF16)

        def two(c):
            return packed.at[g, pl.ds(pl.multiple_of(c * 2 * TILE, 2 * TILE), 2 * TILE), :]

        @pl.loop(1, CHIPS)
        def _(j):
            to = lax.rem(chip + j, CHIPS)
            pltpu.make_async_remote_copy(
                src_ref=two(to), dst_ref=landed.at[g, chip], send_sem=out_send.at[g], recv_sem=out_recv.at[g],
                device_id=(2 * to + core, tp), device_id_type=MESH,
            ).start()

        pltpu.make_async_copy(two(chip), landed.at[g, chip], out_recv.at[g]).start()

    @pl.when(row != tp)
    def _():
        pltpu.make_async_copy(places, places, place_recv).wait()

    goal = places[...]

    @pl.loop(0, GROUP * ROWS, step=64)
    def _(base):
        base = pl.multiple_of(base, 64)
        rows = iota((64, N_DC * TILE), 0) + base
        unpack[pl.ds(base, 64), :] = jnp.where(rows == goal, 1.0, 0.0).astype(BF16)

    def hand(g):
        its = pl.ds(pl.multiple_of((1 - core) * TILE, TILE), TILE)
        return pltpu.make_async_remote_copy(
            src_ref=landed.at[g, :, its, :], dst_ref=handed.at[g], send_sem=hand_send.at[g], recv_sem=hand_recv.at[g],
            device_id=(sibling, tp), device_id_type=MESH,
        )

    def written(g):
        part_of = pl.ds(g * GROUP * HEAD_DIM, GROUP * HEAD_DIM)
        return pltpu.make_async_copy(attended.at[:, part_of], out_ref.at[:, part_of], out_sem.at[g])

    ours = pl.ds(pl.multiple_of(core * TILE, TILE), TILE)
    for g in every:
        pltpu.make_async_copy(landed.at[g], landed.at[g], out_recv.at[g]).wait()
        hand(g).start()
        half = N_DC * TILE // 2
        rows = jnp.dot(unpack[:, :half], landed[g, :, ours, :].reshape(half, HEAD_DIM), preferred_element_type=F32)
        hand(g).wait_recv()
        rows = rows + jnp.dot(unpack[:, half:], handed[g].reshape(half, HEAD_DIM), preferred_element_type=F32)
        rows = rows.astype(BF16)
        for i in range(GROUP):
            h = g * GROUP + i
            attended[:, h * HEAD_DIM : (h + 1) * HEAD_DIM] = rows[i * ROWS : (i + 1) * ROWS]
        written(g).start()

    seven = kin.at[pl.ds(0, ROWS - 16), :]
    pltpu.make_async_copy(seven, seven, kv_send.at[0]).wait()
    pltpu.make_async_copy(seven, seven, kv_send.at[1]).wait()
    sent = qin.at[pl.ds(0, ROWS - 16), :]
    pltpu.make_async_copy(sent, sent, q_send).wait()
    for i in range(COLS):
        pl.when(tp * COLS + i != chip)(pltpu.make_async_copy(own_ref, own_ref, own_send.at[i]).wait)

    @pl.when(row == tp)
    def _():
        @pl.loop(1, N_TP)
        def _(j):
            pltpu.make_async_copy(places, places, place_send.at[j]).wait()

    def left(copies):
        for needed, copy in copies:
            pl.when(needed)(copy.wait_send)

    for p in range(len(PARTS)):
        for j in range(REACH // 2 // COLS + 1):
            left(down(j, p))
            left([along(j, s, p) for s in sideways(j)])
            left(below(j, p))

        @pl.loop(0, REACH // 2 + 1)
        def _(k):
            gone = rows_of(2 * k, p)
            passed = (k <= chip) & jnp.where(core == 0, k < REACH // 2, k > 0)
            pl.when(passed)(lambda: pltpu.make_async_copy(gone, gone, across_send.at[k, p]).wait())

    for g in range(PER // GROUP):
        sent = landed.at[g, pl.ds(0, CHIPS - 1)]
        pltpu.make_async_copy(sent, sent, out_send.at[g]).wait()
        hand(g).wait_send()
        written(g).wait()


def per_device(queries, keys, values, document_index, owner):
    hbm = pl.BlockSpec(memory_space=pltpu.HBM)
    dma = pltpu.SemaphoreType.DMA
    groups, parts = PER // GROUP, len(PARTS)
    return pl.pallas_call(
        kernel,
        out_shape=jax.ShapeDtypeStruct((ROWS, PER * HEAD_DIM), BF16),
        in_specs=[hbm] * 5,
        out_specs=hbm,
        scratch_shapes=[
            pltpu.VMEM((ROWS, HEAD_DIM), BF16),
            pltpu.VMEM((ROWS, PER * HEAD_DIM), BF16),
            pltpu.VMEM((SLOTS, END, ROWS), BF16),
            pltpu.VMEM((ROWS, ROWS), BF16),
            pltpu.VMEM((PER * ROWS, 2 * HEAD_DIM), BF16),
            pltpu.VMEM((PER * ROWS, ROWS), F32),
            pltpu.VMEM((PER * ROWS, ROWS), F32),
            pltpu.VMEM((PER * ROWS, HEAD_DIM), F32),
            pltpu.VMEM((N_DC * TILE, GROUP * ROWS), BF16),
            pltpu.VMEM((GROUP * ROWS, N_DC * TILE), BF16),
            pltpu.VMEM((groups, N_DC * TILE, HEAD_DIM), BF16),
            pltpu.VMEM((groups, CHIPS, 2 * TILE, HEAD_DIM), BF16),
            pltpu.VMEM((groups, CHIPS, TILE, HEAD_DIM), BF16),
            pltpu.VMEM((ROWS, PER * HEAD_DIM), BF16),
            pltpu.VMEM((2, CHIPS, 1, ROWS), I32),
            pltpu.VMEM((1, N_DC * TILE), I32),
            pltpu.VMEM((1, ROWS), I32),
            pltpu.VMEM((1, ROWS), I32),
            dma((2,)), dma((2,)), dma, dma, dma((COLS + 1,)), dma((2,)), dma((N_TP,)), dma, dma((2,)),
            dma((4, parts)), dma((4, parts)), dma((5, 7, parts)), dma((REACH // 2 + 1, parts)), dma((SLOTS, parts)), dma((groups,)), dma((groups,)),
            dma((groups,)), dma((groups,)), dma((groups,)), pltpu.SemaphoreType.REGULAR((3,)),
        ],
        compiler_params=pltpu.CompilerParams(
            collective_id=0, has_side_effects=True, vmem_limit_bytes=63 * 1024 * 1024
        ),
        cost_estimate=pl.CostEstimate(flops=2_300_000_000, bytes_accessed=4_000_000, transcendentals=4_500_000),
    )(queries, keys, values, document_index.reshape(1, ROWS), owner.reshape(1, ROWS))


def solution(mesh):
    return jax.shard_map(
        per_device,
        mesh=mesh,
        in_specs=(
            P(("dc", "tp"), None),
            P(("dc", "tp"), None),
            P(("dc", "tp"), None),
            P("dc"),
            P("dc"),
        ),
        out_specs=P("dc", "tp"),
        check_vma=False,
    )
```

```python
import functools
import math

import jax
import jax.numpy as jnp
from jax import lax
from jax.experimental import pallas as pl
from jax.experimental.pallas import tpu as pltpu
from jax.sharding import PartitionSpec as P

MESH = pl.DeviceIdType.MESH
HEADS = 64
KVH = 8
HEAD_DIM = 128
ROWS = 128
N_DC = 64
N_TP = 8
ROWS_OF_CHIPS, COLS = 8, 4
CHIPS = ROWS_OF_CHIPS * COLS
PER = HEADS // KVH
REACH = 32
SLOTS = 34
STEP = 8
CAP = 4
GROUP = 4
TILE = CAP * GROUP
DEAD = -1e30
V0, K0, D0, Z0, END = 0, 128, 256, 272, 384
PARTS = ((K0, Z0), (V0, K0))
DOWN = {0: (1,), 1: (1,), 2: (1,), 3: (1,)}
VALUES = 1
SCALE = math.log2(math.e) / math.sqrt(HEAD_DIM)
F32, BF16, I32 = jnp.float32, jnp.bfloat16, jnp.int32


def iota(shape, dim):
    return lax.broadcasted_iota(I32, shape, dim)


def kernel(
    q_hbm, k_hbm, v_hbm, doc_hbm, own_hbm, out_ref,
    kin, qin, slots, neg, queries, peak, totals, weighted, pack, unpack, packed, landed, handed, owners, places, doc_ref, own_ref,
    kv_send, kv_recv, q_send, q_recv, own_send, own_recv, place_send, place_recv, doc_sem, down_send, below_send, along_send, across_send, spread_recv, out_send, out_recv, hand_send, hand_recv, heard,
):
    me = lax.axis_index("dc")
    tp = lax.axis_index("tp")

    pltpu.make_async_copy(doc_hbm, doc_ref, doc_sem.at[0]).start()
    pltpu.make_async_copy(own_hbm, own_ref, doc_sem.at[1]).start()
    chip, core = me // 2, lax.rem(me, 2)
    row, col = chip // COLS, lax.rem(chip, COLS)
    sibling = me + 1 - 2 * core

    def rows_on(n):
        return lax.rem(row + n + ROWS_OF_CHIPS, ROWS_OF_CHIPS) * 2 * COLS + 2 * col + core

    def greet(semaphore, device):
        pl.semaphore_signal(semaphore, inc=1, device_id=device, device_id_type=MESH)

    barrier = pltpu.get_barrier_semaphore()

    @pl.loop(1, N_TP)
    def _(j):
        greet(barrier, (me, lax.rem(tp + j, N_TP)))

    greet(barrier, (sibling, tp))
    for n in range(1, COLS):
        greet(barrier, (row * 2 * COLS + 2 * lax.rem(col + n, COLS) + core, tp))
    for n in (-1, 1):
        greet(barrier, (rows_on(n), tp))
    pl.semaphore_wait(barrier, N_TP - 1 + 1 + COLS - 1 + 2)

    def tell(stage):
        if stage == 2:
            greet(heard.at[2], (rows_on(4), tp))
        else:
            greet(heard.at[stage], (rows_on(stage + 1), tp))
            greet(heard.at[stage], (rows_on(-stage - 1), tp))

    def hear(stage):
        pl.semaphore_wait(heard.at[stage], 1 if stage == 2 else 2)

    tell(0)

    mine = pl.ds(pl.multiple_of(tp * 16, 16), 16)

    def columns(t, width):
        return pl.ds(pl.multiple_of(t * width, width), width)

    def part(source, t, width, target, send, recv):
        return pltpu.make_async_remote_copy(
            src_ref=source.at[:, columns(t, width)], dst_ref=target, send_sem=send, recv_sem=recv,
            device_id=(me, t), device_id_type=MESH,
        )

    value_target = slots.at[0, pl.ds(pl.multiple_of(V0 + tp * 16, 16), 16), :]

    @pl.loop(1, N_TP)
    def _(j):
        t = lax.rem(tp + j, N_TP)
        part(k_hbm, t, HEAD_DIM, kin.at[mine, :], kv_send.at[0], kv_recv.at[0]).start()
        part(v_hbm, t, HEAD_DIM, value_target, kv_send.at[1], kv_recv.at[1]).start()

    pltpu.make_async_copy(k_hbm.at[:, columns(tp, HEAD_DIM)], kin.at[mine, :], kv_recv.at[0]).start()
    pltpu.make_async_copy(v_hbm.at[:, columns(tp, HEAD_DIM)], value_target, kv_recv.at[1]).start()

    @pl.loop(1, N_TP)
    def _(j):
        t = lax.rem(tp + j, N_TP)
        part(q_hbm, t, PER * HEAD_DIM, qin.at[mine, :], q_send, q_recv).start()

    pltpu.make_async_copy(q_hbm.at[:, columns(tp, PER * HEAD_DIM)], qin.at[mine, :], q_recv).start()

    slots[:, Z0:END, :] = jnp.zeros((SLOTS, END - Z0, ROWS), BF16)
    reach = jnp.minimum(me, REACH)

    @pl.loop(reach + 1, jnp.minimum((reach // STEP + 1) * STEP, SLOTS))
    def _(r):
        slots[r, V0:D0, :] = jnp.zeros((D0 - V0, ROWS), BF16)
        slots[r, D0:Z0, :] = jnp.ones((Z0 - D0, ROWS), BF16)

    pltpu.make_async_copy(doc_hbm, doc_ref, doc_sem.at[0]).wait()
    doc = doc_ref[...]
    slots[0, D0:Z0, :] = jnp.where(iota((Z0 - D0, ROWS), 0) == doc, 1.0, 0.0).astype(BF16)
    other = jnp.where((iota((ROWS, ROWS), 0) != doc) & (iota((ROWS, ROWS), 0) < Z0 - D0), DEAD, 0.0)
    neg[...] = other.T.astype(BF16)

    pltpu.make_async_copy(own_hbm, own_ref, doc_sem.at[1]).wait()
    owner = own_ref[...]
    owner_col = jnp.broadcast_to(owner, (ROWS, ROWS)).astype(F32).T
    same = (owner_col == owner.astype(F32)) & (iota((ROWS, ROWS), 0) < iota((ROWS, ROWS), 1))
    rank = jnp.sum(jnp.where(same, 1.0, 0.0), axis=0, keepdims=True).astype(I32)
    place = owner * TILE + rank
    target = jnp.concatenate([place + h * CAP for h in range(GROUP)], axis=1)

    @pl.loop(0, N_DC * TILE, step=128)
    def _(base):
        base = pl.multiple_of(base, 128)
        rows = iota((128, GROUP * ROWS), 0) + base
        pack[pl.ds(base, 128), :] = jnp.where(rows == target, 1.0, 0.0).astype(BF16)

    hear(0)
    tell(1)

    pltpu.make_async_copy(kin, kin, kv_recv.at[0]).wait()
    slots[0, K0:D0, :] = kin[...].astype(F32).T.astype(BF16)

    def rows_of(r, p):
        return slots.at[r, pl.ds(PARTS[p][0], PARTS[p][1] - PARTS[p][0]), :]

    def send(r, target, r_there, sem, p):
        return pltpu.make_async_remote_copy(
            src_ref=rows_of(r, p), dst_ref=rows_of(r_there, p), send_sem=sem.at[p],
            recv_sem=spread_recv.at[r_there, p], device_id=(target, tp), device_id_type=MESH,
        )

    def arrived(r, p):
        pltpu.make_async_copy(rows_of(r, p), rows_of(r, p), spread_recv.at[r, p]).wait()

    def down(j, p):
        found = []
        for n in DOWN.get(j, ()):
            there = 2 * COLS * (j + n)
            copy = send(2 * COLS * j, me + 2 * COLS * n, there, down_send.at[j + n - 1], p)
            found.append(((row >= j) & (row + n < ROWS_OF_CHIPS), copy))
        return found

    def along(j, step, p):
        k = COLS * j + step
        return (row >= j) & (col + step >= 0) & (col + step < COLS), send(
            2 * COLS * j, me + 2 * step, 2 * k, along_send.at[j, step + COLS - 1], p
        )

    def steps(j):
        return [s for s in range(1 - COLS, COLS) if s and 0 < COLS * j + s <= REACH // 2]

    def sideways(j):
        return [s for s in steps(j) if abs(s) != 2 or j < 2]

    def below(j, p):
        found = []
        for s in (2, -2):
            k = COLS * j + s
            if j and k + COLS <= REACH // 2:
                copy = send(2 * k, me + 2 * COLS, 2 * (k + COLS), below_send.at[j], p)
                there = (row >= j) & (row < ROWS_OF_CHIPS - 1) & (col - s >= 0) & (col - s < COLS)
                found.append((there, copy))
        return found

    def across(k, p):
        found = []
        if k < REACH // 2:
            found.append((core == 0, send(2 * k, me + 1, 2 * k + 1, across_send.at[k], p)))
        if k > 0:
            found.append((core == 1, send(2 * k, me - 1, 2 * k - 1, across_send.at[k], p)))
        return found

    def start(copies):
        for needed, copy in copies:
            pl.when(needed)(copy.start)

    def from_column(j):
        for p in range(len(PARTS)):
            if j:
                pl.when(row >= j)(functools.partial(arrived, 2 * COLS * j, p))
            elif p == VALUES:
                pltpu.make_async_copy(kin, kin, kv_recv.at[1]).wait()
            start(down(j, p))
            start([along(j, s, p) for s in sideways(j)])
            start([((row >= j) & its_core, copy) for its_core, copy in across(COLS * j, p)])

    def from_row(j):
        for p in range(len(PARTS)):
            for s in sorted(steps(j), key=lambda s: abs(s) != 2):
                k = COLS * j + s

                @pl.when((row >= j) & (col - s >= 0) & (col - s < COLS))
                def _():
                    arrived(2 * k, p)
                    if abs(s) == 2:
                        start(below(j, p))
                    start(across(k, p))

    from_column(0)

    def send_owner():
        for i in range(COLS):
            there = tp * COLS + i
            pl.when(there != chip)(pltpu.make_async_remote_copy(
                src_ref=own_ref, dst_ref=owners.at[core, chip], send_sem=own_send.at[i], recv_sem=own_recv.at[0],
                device_id=(2 * there + core, tp), device_id_type=MESH,
            ).start)
        pl.when(row == tp)(pltpu.make_async_copy(own_ref, owners.at[core, chip], own_recv.at[0]).start)

    def swap_owners():
        return pltpu.make_async_remote_copy(
            src_ref=owners.at[core], dst_ref=owners.at[core], send_sem=own_send.at[COLS], recv_sem=own_recv.at[1],
            device_id=(sibling, tp), device_id_type=MESH,
        )

    def gather_owners():
        pltpu.make_async_copy(owners.at[core], owners.at[core], own_recv.at[0]).wait()
        swap_owners().start()

    def send_places():
        swap_owners().wait()
        hits = jnp.where(owners[...].reshape(N_DC, ROWS) == me, 1.0, 0.0).astype(BF16)
        counts = lax.dot_general(
            jnp.ones((8, ROWS), BF16), hits, (((1,), (1,)), ((), ())), preferred_element_type=F32
        ).astype(BF16)
        lane = iota((1, N_DC * TILE), 1)
        turn = lax.rem(lane, CAP)
        from_core = jnp.where(lane < N_DC * TILE // 2, core, 1 - core)
        source = 2 * lax.rem(lane // TILE, CHIPS) + from_core
        listed = iota((N_DC, N_DC * TILE), 0)
        listed = 2 * lax.rem(listed, CHIPS) + listed // CHIPS
        count = jnp.dot(counts, jnp.where(listed == source, 1.0, 0.0).astype(BF16), preferred_element_type=F32)
        before = jnp.dot(counts, jnp.where(listed < source, 1.0, 0.0).astype(BF16), preferred_element_type=F32)
        head = lax.rem(lane // CAP, GROUP)
        places[...] = jnp.where(turn < count[0:1].astype(I32), before[0:1].astype(I32) + turn + head * ROWS, -1)

        @pl.loop(1, N_TP)
        def _(j):
            pltpu.make_async_remote_copy(
                src_ref=places, dst_ref=places, send_sem=place_send.at[j], recv_sem=place_recv,
                device_id=(me, lax.rem(tp + j, N_TP)), device_id_type=MESH,
            ).start()

    def arrive(r):
        @pl.when((lax.rem(r, 2) == 1) & (r <= reach))
        def _():
            for p in range(len(PARTS)):
                arrived(r, p)

    def attend(step, group):
        base = step * STEP
        count = min(STEP, SLOTS - base)
        at = pl.ds(group * GROUP * ROWS, GROUP * ROWS)
        keys = jnp.concatenate([slots[base + i, K0:END, :] for i in range(count)], axis=1)
        values = jnp.concatenate([slots[base + i, V0:K0, :] for i in range(count)], axis=0)
        s = jnp.dot(queries[at, :], keys, preferred_element_type=F32)
        s = [s[:, i * ROWS : (i + 1) * ROWS] for i in range(count)]
        if step == 0:
            row_of = lax.rem(iota((GROUP * ROWS, ROWS), 0), ROWS)
            s[0] = jnp.where(iota((GROUP * ROWS, ROWS), 1) <= row_of, s[0], DEAD)
        top = jnp.max(functools.reduce(jnp.maximum, s), axis=1, keepdims=True)
        if step == 0:
            top = jnp.broadcast_to(top, (GROUP * ROWS, ROWS))
        else:
            old = peak[at, :]
            top = jnp.maximum(old, top)
            shrink = jnp.exp2((old - top) * SCALE)
        weights = [jnp.exp2((x - top) * SCALE) for x in s]
        total = functools.reduce(jnp.add, weights)
        rounded = jnp.concatenate([w.astype(BF16) for w in weights], axis=1)
        summed = jnp.dot(rounded, values, preferred_element_type=F32)
        if step > 0:
            total = totals[at, :] * shrink + total
            summed = weighted[at, :] * shrink + summed
        peak[at, :] = top
        totals[at, :] = total
        weighted[at, :] = summed

    def step_of(step, groups):
        def run():
            for i in range(1, min(STEP, SLOTS - step * STEP), 2):
                if groups[0] == 0:
                    arrive(jnp.int32(step * STEP + i))
            for g in groups:
                attend(step, g)

        if step:
            pl.when(reach >= step * STEP)(run)
        else:
            run()

    every = tuple(range(PER // GROUP))
    from_column(1)
    hear(1)
    tell(2)
    from_row(0)
    from_column(2)
    from_row(1)
    hear(2)
    from_column(3)
    from_row(2)
    pltpu.make_async_copy(qin, qin, q_recv).wait()
    for h in range(PER):
        queries[h * ROWS : (h + 1) * ROWS, :HEAD_DIM] = qin[:, h * HEAD_DIM : (h + 1) * HEAD_DIM]
        queries[h * ROWS : (h + 1) * ROWS, HEAD_DIM:] = neg[...]
    from_column(4)
    from_row(3)
    send_owner()
    step_of(0, (0,))
    step_of(0, (1,))
    from_row(4)
    pl.when(row == tp)(gather_owners)
    step_of(1, (0,))
    step_of(1, (1,))
    pl.when(row == tp)(send_places)
    step_of(2, (0,))
    step_of(2, (1,))

    for g in every:
        step_of(3, (g,))
        step_of(4, (g,))
        at = pl.ds(g * GROUP * ROWS, GROUP * ROWS)
        context = (weighted[at, :] / jnp.sum(totals[at, :], axis=1, keepdims=True)).astype(BF16)
        packed[g] = jnp.dot(pack[...], context, preferred_element_type=F32).astype(BF16)

        def two(c):
            return packed.at[g, pl.ds(pl.multiple_of(c * 2 * TILE, 2 * TILE), 2 * TILE), :]

        @pl.loop(1, CHIPS)
        def _(j):
            to = lax.rem(chip + j, CHIPS)
            pltpu.make_async_remote_copy(
                src_ref=two(to), dst_ref=landed.at[g, chip], send_sem=out_send.at[g], recv_sem=out_recv.at[g],
                device_id=(2 * to + core, tp), device_id_type=MESH,
            ).start()

        pltpu.make_async_copy(two(chip), landed.at[g, chip], out_recv.at[g]).start()

    @pl.when(row != tp)
    def _():
        pltpu.make_async_copy(places, places, place_recv).wait()

    goal = places[...]

    @pl.loop(0, GROUP * ROWS, step=64)
    def _(base):
        base = pl.multiple_of(base, 64)
        rows = iota((64, N_DC * TILE), 0) + base
        unpack[pl.ds(base, 64), :] = jnp.where(rows == goal, 1.0, 0.0).astype(BF16)

    def hand(g):
        its = pl.ds(pl.multiple_of((1 - core) * TILE, TILE), TILE)
        return pltpu.make_async_remote_copy(
            src_ref=landed.at[g, :, its, :], dst_ref=handed.at[g], send_sem=hand_send.at[g], recv_sem=hand_recv.at[g],
            device_id=(sibling, tp), device_id_type=MESH,
        )

    ours = pl.ds(pl.multiple_of(core * TILE, TILE), TILE)
    for g in every:
        pltpu.make_async_copy(landed.at[g], landed.at[g], out_recv.at[g]).wait()
        hand(g).start()
        half = N_DC * TILE // 2
        rows = jnp.dot(unpack[:, :half], landed[g, :, ours, :].reshape(half, HEAD_DIM), preferred_element_type=F32)
        hand(g).wait_recv()
        rows = rows + jnp.dot(unpack[:, half:], handed[g].reshape(half, HEAD_DIM), preferred_element_type=F32)
        rows = rows.astype(BF16)
        for i in range(GROUP):
            h = g * GROUP + i
            out_ref[:, h * HEAD_DIM : (h + 1) * HEAD_DIM] = rows[i * ROWS : (i + 1) * ROWS]

    seven = kin.at[pl.ds(0, ROWS - 16), :]
    pltpu.make_async_copy(seven, seven, kv_send.at[0]).wait()
    pltpu.make_async_copy(seven, seven, kv_send.at[1]).wait()
    sent = qin.at[pl.ds(0, ROWS - 16), :]
    pltpu.make_async_copy(sent, sent, q_send).wait()
    for i in range(COLS):
        pl.when(tp * COLS + i != chip)(pltpu.make_async_copy(own_ref, own_ref, own_send.at[i]).wait)

    @pl.when(row == tp)
    def _():
        @pl.loop(1, N_TP)
        def _(j):
            pltpu.make_async_copy(places, places, place_send.at[j]).wait()

    def left(copies):
        for needed, copy in copies:
            pl.when(needed)(copy.wait_send)

    for p in range(len(PARTS)):
        for j in range(REACH // 2 // COLS + 1):
            left(down(j, p))
            left([along(j, s, p) for s in sideways(j)])
            left(below(j, p))

        @pl.loop(0, REACH // 2 + 1)
        def _(k):
            gone = rows_of(2 * k, p)
            passed = (k <= chip) & jnp.where(core == 0, k < REACH // 2, k > 0)
            pl.when(passed)(lambda: pltpu.make_async_copy(gone, gone, across_send.at[k, p]).wait())

    for g in range(PER // GROUP):
        sent = landed.at[g, pl.ds(0, CHIPS - 1)]
        pltpu.make_async_copy(sent, sent, out_send.at[g]).wait()
        hand(g).wait_send()


def per_device(queries, keys, values, document_index, owner):
    hbm = pl.BlockSpec(memory_space=pltpu.HBM)
    dma = pltpu.SemaphoreType.DMA
    operands = (queries, keys, values, document_index.reshape(1, ROWS), owner.reshape(1, ROWS))
    groups, parts = PER // GROUP, len(PARTS)
    return pl.pallas_call(
        kernel,
        out_shape=jax.ShapeDtypeStruct((ROWS, PER * HEAD_DIM), BF16),
        in_specs=[hbm] * 5,
        out_specs=pl.BlockSpec(memory_space=pltpu.VMEM),
        scratch_shapes=[
            pltpu.VMEM((ROWS, HEAD_DIM), BF16),
            pltpu.VMEM((ROWS, PER * HEAD_DIM), BF16),
            pltpu.VMEM((SLOTS, END, ROWS), BF16),
            pltpu.VMEM((ROWS, ROWS), BF16),
            pltpu.VMEM((PER * ROWS, 2 * HEAD_DIM), BF16),
            pltpu.VMEM((PER * ROWS, ROWS), F32),
            pltpu.VMEM((PER * ROWS, ROWS), F32),
            pltpu.VMEM((PER * ROWS, HEAD_DIM), F32),
            pltpu.VMEM((N_DC * TILE, GROUP * ROWS), BF16),
            pltpu.VMEM((GROUP * ROWS, N_DC * TILE), BF16),
            pltpu.VMEM((groups, N_DC * TILE, HEAD_DIM), BF16),
            pltpu.VMEM((groups, CHIPS, 2 * TILE, HEAD_DIM), BF16),
            pltpu.VMEM((groups, CHIPS, TILE, HEAD_DIM), BF16),
            pltpu.VMEM((2, CHIPS, 1, ROWS), I32),
            pltpu.VMEM((1, N_DC * TILE), I32),
            pltpu.VMEM((1, ROWS), I32),
            pltpu.VMEM((1, ROWS), I32),
            dma((2,)), dma((2,)), dma, dma, dma((COLS + 1,)), dma((2,)), dma((N_TP,)), dma, dma((2,)),
            dma((4, parts)), dma((4, parts)), dma((5, 7, parts)), dma((REACH // 2 + 1, parts)), dma((SLOTS, parts)), dma((groups,)), dma((groups,)),
            dma((groups,)), dma((groups,)), pltpu.SemaphoreType.REGULAR((3,)),
        ],
        compiler_params=pltpu.CompilerParams(
            collective_id=0, has_side_effects=True, vmem_limit_bytes=48 * 1024 * 1024
        ),
        cost_estimate=pl.CostEstimate(flops=2_300_000_000, bytes_accessed=4_000_000, transcendentals=4_500_000),
    )(*(pltpu.with_memory_space_constraint(x, pltpu.HBM) for x in operands))


def solution(mesh):
    return jax.shard_map(
        per_device,
        mesh=mesh,
        in_specs=(
            P(("dc", "tp"), None),
            P(("dc", "tp"), None),
            P(("dc", "tp"), None),
            P("dc"),
            P("dc"),
        ),
        out_specs=P("dc", "tp"),
        check_vma=False,
    )
```

```python
import functools
import math

import jax
import jax.numpy as jnp
from jax import lax
from jax.experimental import pallas as pl
from jax.experimental.pallas import tpu as pltpu
from jax.sharding import PartitionSpec as P

MESH = pl.DeviceIdType.MESH
HEADS = 64
KVH = 8
HEAD_DIM = 128
ROWS = 128
N_DC = 64
N_TP = 8
ROWS_OF_CHIPS, COLS = 8, 4
CHIPS = ROWS_OF_CHIPS * COLS
PER = HEADS // KVH
REACH = 32
SLOTS = 34
STEP = 8
CAP = 4
GROUP = 4
TILE = CAP * GROUP
DEAD = -1e30
V0, K0, D0, Z0, END = 0, 128, 256, 272, 384
PARTS = ((K0, Z0), (V0, K0))
DOWN = {0: (1,), 1: (1,), 2: (1,), 3: (1,)}
VALUES = 1
SCALE = math.log2(math.e) / math.sqrt(HEAD_DIM)
F32, BF16, I32 = jnp.float32, jnp.bfloat16, jnp.int32


def iota(shape, dim):
    return lax.broadcasted_iota(I32, shape, dim)


def kernel(
    q_hbm, k_hbm, v_hbm, doc_hbm, own_hbm, out_ref,
    k_near, v_near, kin, qin, slots, neg, queries, peak, totals, weighted, pack, unpack, packed, landed, handed, owners, places, doc_ref, own_ref,
    stage_sem, kv_send, kv_recv, q_send, q_recv, own_send, own_recv, place_send, place_recv, doc_sem, down_send, below_send, along_send, across_send, spread_recv, out_send, out_recv, hand_send, hand_recv, heard,
):
    me = lax.axis_index("dc")
    tp = lax.axis_index("tp")

    staged = [
        pltpu.make_async_copy(k_hbm, k_near, stage_sem.at[0]),
        pltpu.make_async_copy(v_hbm, v_near, stage_sem.at[1]),
    ]
    for copy in staged:
        copy.start()
    pltpu.make_async_copy(doc_hbm, doc_ref, doc_sem.at[0]).start()
    pltpu.make_async_copy(own_hbm, own_ref, doc_sem.at[1]).start()
    chip, core = me // 2, lax.rem(me, 2)
    row, col = chip // COLS, lax.rem(chip, COLS)
    sibling = me + 1 - 2 * core

    def rows_on(n):
        return lax.rem(row + n + ROWS_OF_CHIPS, ROWS_OF_CHIPS) * 2 * COLS + 2 * col + core

    def greet(semaphore, device):
        pl.semaphore_signal(semaphore, inc=1, device_id=device, device_id_type=MESH)

    barrier = pltpu.get_barrier_semaphore()

    @pl.loop(1, N_TP)
    def _(j):
        greet(barrier, (me, lax.rem(tp + j, N_TP)))

    greet(barrier, (sibling, tp))
    for n in range(1, COLS):
        greet(barrier, (row * 2 * COLS + 2 * lax.rem(col + n, COLS) + core, tp))
    for n in (-1, 1):
        greet(barrier, (rows_on(n), tp))
    pl.semaphore_wait(barrier, N_TP - 1 + 1 + COLS - 1 + 2)

    def tell(stage):
        if stage == 2:
            greet(heard.at[2], (rows_on(4), tp))
        else:
            greet(heard.at[stage], (rows_on(stage + 1), tp))
            greet(heard.at[stage], (rows_on(-stage - 1), tp))

    def hear(stage):
        pl.semaphore_wait(heard.at[stage], 1 if stage == 2 else 2)

    tell(0)

    mine = pl.ds(pl.multiple_of(tp * 16, 16), 16)

    def columns(t, width):
        return pl.ds(pl.multiple_of(t * width, width), width)

    def part(source, t, width, target, send, recv):
        return pltpu.make_async_remote_copy(
            src_ref=source.at[:, columns(t, width)], dst_ref=target, send_sem=send, recv_sem=recv,
            device_id=(me, t), device_id_type=MESH,
        )

    for copy in staged:
        copy.wait()
    value_target = slots.at[0, pl.ds(pl.multiple_of(V0 + tp * 16, 16), 16), :]

    @pl.loop(1, N_TP)
    def _(j):
        t = lax.rem(tp + j, N_TP)
        part(k_near, t, HEAD_DIM, kin.at[mine, :], kv_send.at[0], kv_recv.at[0]).start()
        part(v_near, t, HEAD_DIM, value_target, kv_send.at[1], kv_recv.at[1]).start()

    pltpu.make_async_copy(k_near.at[:, columns(tp, HEAD_DIM)], kin.at[mine, :], kv_recv.at[0]).start()
    pltpu.make_async_copy(v_near.at[:, columns(tp, HEAD_DIM)], value_target, kv_recv.at[1]).start()

    @pl.loop(1, N_TP)
    def _(j):
        t = lax.rem(tp + j, N_TP)
        part(q_hbm, t, PER * HEAD_DIM, qin.at[mine, :], q_send, q_recv).start()

    pltpu.make_async_copy(q_hbm.at[:, columns(tp, PER * HEAD_DIM)], qin.at[mine, :], q_recv).start()

    slots[:, Z0:END, :] = jnp.zeros((SLOTS, END - Z0, ROWS), BF16)
    reach = jnp.minimum(me, REACH)

    @pl.loop(reach + 1, jnp.minimum((reach // STEP + 1) * STEP, SLOTS))
    def _(r):
        slots[r, V0:D0, :] = jnp.zeros((D0 - V0, ROWS), BF16)
        slots[r, D0:Z0, :] = jnp.ones((Z0 - D0, ROWS), BF16)

    pltpu.make_async_copy(doc_hbm, doc_ref, doc_sem.at[0]).wait()
    doc = doc_ref[...]
    slots[0, D0:Z0, :] = jnp.where(iota((Z0 - D0, ROWS), 0) == doc, 1.0, 0.0).astype(BF16)
    other = jnp.where((iota((ROWS, ROWS), 0) != doc) & (iota((ROWS, ROWS), 0) < Z0 - D0), DEAD, 0.0)
    neg[...] = other.T.astype(BF16)

    pltpu.make_async_copy(own_hbm, own_ref, doc_sem.at[1]).wait()
    owner = own_ref[...]
    owner_col = jnp.broadcast_to(owner, (ROWS, ROWS)).astype(F32).T
    same = (owner_col == owner.astype(F32)) & (iota((ROWS, ROWS), 0) < iota((ROWS, ROWS), 1))
    rank = jnp.sum(jnp.where(same, 1.0, 0.0), axis=0, keepdims=True).astype(I32)
    place = owner * TILE + rank
    target = jnp.concatenate([place + h * CAP for h in range(GROUP)], axis=1)

    @pl.loop(0, N_DC * TILE, step=128)
    def _(base):
        base = pl.multiple_of(base, 128)
        rows = iota((128, GROUP * ROWS), 0) + base
        pack[pl.ds(base, 128), :] = jnp.where(rows == target, 1.0, 0.0).astype(BF16)

    hear(0)
    tell(1)

    pltpu.make_async_copy(kin, kin, kv_recv.at[0]).wait()
    slots[0, K0:D0, :] = kin[...].astype(F32).T.astype(BF16)

    def rows_of(r, p):
        return slots.at[r, pl.ds(PARTS[p][0], PARTS[p][1] - PARTS[p][0]), :]

    def send(r, target, r_there, sem, p):
        return pltpu.make_async_remote_copy(
            src_ref=rows_of(r, p), dst_ref=rows_of(r_there, p), send_sem=sem.at[p],
            recv_sem=spread_recv.at[r_there, p], device_id=(target, tp), device_id_type=MESH,
        )

    def arrived(r, p):
        pltpu.make_async_copy(rows_of(r, p), rows_of(r, p), spread_recv.at[r, p]).wait()

    def down(j, p):
        found = []
        for n in DOWN.get(j, ()):
            there = 2 * COLS * (j + n)
            copy = send(2 * COLS * j, me + 2 * COLS * n, there, down_send.at[j + n - 1], p)
            found.append(((row >= j) & (row + n < ROWS_OF_CHIPS), copy))
        return found

    def along(j, step, p):
        k = COLS * j + step
        return (row >= j) & (col + step >= 0) & (col + step < COLS), send(
            2 * COLS * j, me + 2 * step, 2 * k, along_send.at[j, step + COLS - 1], p
        )

    def steps(j):
        return [s for s in range(1 - COLS, COLS) if s and 0 < COLS * j + s <= REACH // 2]

    def sideways(j):
        return [s for s in steps(j) if abs(s) != 2 or j < 2]

    def below(j, p):
        found = []
        for s in (2, -2):
            k = COLS * j + s
            if j and k + COLS <= REACH // 2:
                copy = send(2 * k, me + 2 * COLS, 2 * (k + COLS), below_send.at[j], p)
                there = (row >= j) & (row < ROWS_OF_CHIPS - 1) & (col - s >= 0) & (col - s < COLS)
                found.append((there, copy))
        return found

    def across(k, p):
        found = []
        if k < REACH // 2:
            found.append((core == 0, send(2 * k, me + 1, 2 * k + 1, across_send.at[k], p)))
        if k > 0:
            found.append((core == 1, send(2 * k, me - 1, 2 * k - 1, across_send.at[k], p)))
        return found

    def start(copies):
        for needed, copy in copies:
            pl.when(needed)(copy.start)

    def from_column(j):
        for p in range(len(PARTS)):
            if j:
                pl.when(row >= j)(functools.partial(arrived, 2 * COLS * j, p))
            elif p == VALUES:
                pltpu.make_async_copy(kin, kin, kv_recv.at[1]).wait()
            start(down(j, p))
            start([along(j, s, p) for s in sideways(j)])
            start([((row >= j) & its_core, copy) for its_core, copy in across(COLS * j, p)])

    def from_row(j):
        for p in range(len(PARTS)):
            for s in sorted(steps(j), key=lambda s: abs(s) != 2):
                k = COLS * j + s

                @pl.when((row >= j) & (col - s >= 0) & (col - s < COLS))
                def _():
                    arrived(2 * k, p)
                    if abs(s) == 2:
                        start(below(j, p))
                    start(across(k, p))

    from_column(0)

    def send_owner():
        for i in range(COLS):
            there = tp * COLS + i
            pl.when(there != chip)(pltpu.make_async_remote_copy(
                src_ref=own_ref, dst_ref=owners.at[core, chip], send_sem=own_send.at[i], recv_sem=own_recv.at[0],
                device_id=(2 * there + core, tp), device_id_type=MESH,
            ).start)
        pl.when(row == tp)(pltpu.make_async_copy(own_ref, owners.at[core, chip], own_recv.at[0]).start)

    def swap_owners():
        return pltpu.make_async_remote_copy(
            src_ref=owners.at[core], dst_ref=owners.at[core], send_sem=own_send.at[COLS], recv_sem=own_recv.at[1],
            device_id=(sibling, tp), device_id_type=MESH,
        )

    def gather_owners():
        pltpu.make_async_copy(owners.at[core], owners.at[core], own_recv.at[0]).wait()
        swap_owners().start()

    def send_places():
        swap_owners().wait()
        hits = jnp.where(owners[...].reshape(N_DC, ROWS) == me, 1.0, 0.0).astype(BF16)
        counts = lax.dot_general(
            jnp.ones((8, ROWS), BF16), hits, (((1,), (1,)), ((), ())), preferred_element_type=F32
        ).astype(BF16)
        lane = iota((1, N_DC * TILE), 1)
        turn = lax.rem(lane, CAP)
        from_core = jnp.where(lane < N_DC * TILE // 2, core, 1 - core)
        source = 2 * lax.rem(lane // TILE, CHIPS) + from_core
        listed = iota((N_DC, N_DC * TILE), 0)
        listed = 2 * lax.rem(listed, CHIPS) + listed // CHIPS
        count = jnp.dot(counts, jnp.where(listed == source, 1.0, 0.0).astype(BF16), preferred_element_type=F32)
        before = jnp.dot(counts, jnp.where(listed < source, 1.0, 0.0).astype(BF16), preferred_element_type=F32)
        head = lax.rem(lane // CAP, GROUP)
        places[...] = jnp.where(turn < count[0:1].astype(I32), before[0:1].astype(I32) + turn + head * ROWS, -1)

        @pl.loop(1, N_TP)
        def _(j):
            pltpu.make_async_remote_copy(
                src_ref=places, dst_ref=places, send_sem=place_send.at[j], recv_sem=place_recv,
                device_id=(me, lax.rem(tp + j, N_TP)), device_id_type=MESH,
            ).start()

    def arrive(r):
        @pl.when((lax.rem(r, 2) == 1) & (r <= reach))
        def _():
            for p in range(len(PARTS)):
                arrived(r, p)

    def attend(step, group):
        base = step * STEP
        count = min(STEP, SLOTS - base)
        at = pl.ds(group * GROUP * ROWS, GROUP * ROWS)
        keys = jnp.concatenate([slots[base + i, K0:END, :] for i in range(count)], axis=1)
        values = jnp.concatenate([slots[base + i, V0:K0, :] for i in range(count)], axis=0)
        s = jnp.dot(queries[at, :], keys, preferred_element_type=F32)
        s = [s[:, i * ROWS : (i + 1) * ROWS] for i in range(count)]
        if step == 0:
            row_of = lax.rem(iota((GROUP * ROWS, ROWS), 0), ROWS)
            s[0] = jnp.where(iota((GROUP * ROWS, ROWS), 1) <= row_of, s[0], DEAD)
        top = jnp.max(functools.reduce(jnp.maximum, s), axis=1, keepdims=True)
        if step == 0:
            top = jnp.broadcast_to(top, (GROUP * ROWS, ROWS))
        else:
            old = peak[at, :]
            top = jnp.maximum(old, top)
            shrink = jnp.exp2((old - top) * SCALE)
        weights = [jnp.exp2((x - top) * SCALE) for x in s]
        total = functools.reduce(jnp.add, weights)
        rounded = jnp.concatenate([w.astype(BF16) for w in weights], axis=1)
        summed = jnp.dot(rounded, values, preferred_element_type=F32)
        if step > 0:
            total = totals[at, :] * shrink + total
            summed = weighted[at, :] * shrink + summed
        peak[at, :] = top
        totals[at, :] = total
        weighted[at, :] = summed

    def step_of(step, groups):
        def run():
            for i in range(1, min(STEP, SLOTS - step * STEP), 2):
                if groups[0] == 0:
                    arrive(jnp.int32(step * STEP + i))
            for g in groups:
                attend(step, g)

        if step:
            pl.when(reach >= step * STEP)(run)
        else:
            run()

    every = tuple(range(PER // GROUP))
    from_column(1)
    hear(1)
    tell(2)
    from_row(0)
    from_column(2)
    from_row(1)
    hear(2)
    from_column(3)
    from_row(2)
    pltpu.make_async_copy(qin, qin, q_recv).wait()
    for h in range(PER):
        queries[h * ROWS : (h + 1) * ROWS, :HEAD_DIM] = qin[:, h * HEAD_DIM : (h + 1) * HEAD_DIM]
        queries[h * ROWS : (h + 1) * ROWS, HEAD_DIM:] = neg[...]
    from_column(4)
    from_row(3)
    send_owner()
    step_of(0, (0,))
    step_of(0, (1,))
    from_row(4)
    pl.when(row == tp)(gather_owners)
    step_of(1, (0,))
    step_of(1, (1,))
    pl.when(row == tp)(send_places)
    step_of(2, (0,))
    step_of(2, (1,))

    for g in every:
        step_of(3, (g,))
        step_of(4, (g,))
        at = pl.ds(g * GROUP * ROWS, GROUP * ROWS)
        context = (weighted[at, :] / jnp.sum(totals[at, :], axis=1, keepdims=True)).astype(BF16)
        packed[g] = jnp.dot(pack[...], context, preferred_element_type=F32).astype(BF16)

        def two(c):
            return packed.at[g, pl.ds(pl.multiple_of(c * 2 * TILE, 2 * TILE), 2 * TILE), :]

        @pl.loop(1, CHIPS)
        def _(j):
            to = lax.rem(chip + j, CHIPS)
            pltpu.make_async_remote_copy(
                src_ref=two(to), dst_ref=landed.at[g, chip], send_sem=out_send.at[g], recv_sem=out_recv.at[g],
                device_id=(2 * to + core, tp), device_id_type=MESH,
            ).start()

        pltpu.make_async_copy(two(chip), landed.at[g, chip], out_recv.at[g]).start()

    @pl.when(row != tp)
    def _():
        pltpu.make_async_copy(places, places, place_recv).wait()

    goal = places[...]

    @pl.loop(0, GROUP * ROWS, step=64)
    def _(base):
        base = pl.multiple_of(base, 64)
        rows = iota((64, N_DC * TILE), 0) + base
        unpack[pl.ds(base, 64), :] = jnp.where(rows == goal, 1.0, 0.0).astype(BF16)

    def hand(g):
        its = pl.ds(pl.multiple_of((1 - core) * TILE, TILE), TILE)
        return pltpu.make_async_remote_copy(
            src_ref=landed.at[g, :, its, :], dst_ref=handed.at[g], send_sem=hand_send.at[g], recv_sem=hand_recv.at[g],
            device_id=(sibling, tp), device_id_type=MESH,
        )

    ours = pl.ds(pl.multiple_of(core * TILE, TILE), TILE)
    for g in every:
        pltpu.make_async_copy(landed.at[g], landed.at[g], out_recv.at[g]).wait()
        hand(g).start()
        half = N_DC * TILE // 2
        rows = jnp.dot(unpack[:, :half], landed[g, :, ours, :].reshape(half, HEAD_DIM), preferred_element_type=F32)
        hand(g).wait_recv()
        rows = rows + jnp.dot(unpack[:, half:], handed[g].reshape(half, HEAD_DIM), preferred_element_type=F32)
        rows = rows.astype(BF16)
        for i in range(GROUP):
            h = g * GROUP + i
            out_ref[:, h * HEAD_DIM : (h + 1) * HEAD_DIM] = rows[i * ROWS : (i + 1) * ROWS]

    seven = kin.at[pl.ds(0, ROWS - 16), :]
    pltpu.make_async_copy(seven, seven, kv_send.at[0]).wait()
    pltpu.make_async_copy(seven, seven, kv_send.at[1]).wait()
    sent = qin.at[pl.ds(0, ROWS - 16), :]
    pltpu.make_async_copy(sent, sent, q_send).wait()
    for i in range(COLS):
        pl.when(tp * COLS + i != chip)(pltpu.make_async_copy(own_ref, own_ref, own_send.at[i]).wait)

    @pl.when(row == tp)
    def _():
        @pl.loop(1, N_TP)
        def _(j):
            pltpu.make_async_copy(places, places, place_send.at[j]).wait()

    def left(copies):
        for needed, copy in copies:
            pl.when(needed)(copy.wait_send)

    for p in range(len(PARTS)):
        for j in range(REACH // 2 // COLS + 1):
            left(down(j, p))
            left([along(j, s, p) for s in sideways(j)])
            left(below(j, p))

        @pl.loop(0, REACH // 2 + 1)
        def _(k):
            gone = rows_of(2 * k, p)
            passed = (k <= chip) & jnp.where(core == 0, k < REACH // 2, k > 0)
            pl.when(passed)(lambda: pltpu.make_async_copy(gone, gone, across_send.at[k, p]).wait())

    for g in range(PER // GROUP):
        sent = landed.at[g, pl.ds(0, CHIPS - 1)]
        pltpu.make_async_copy(sent, sent, out_send.at[g]).wait()
        hand(g).wait_send()


def per_device(queries, keys, values, document_index, owner):
    hbm = pl.BlockSpec(memory_space=pltpu.HBM)
    dma = pltpu.SemaphoreType.DMA
    operands = (queries, keys, values, document_index.reshape(1, ROWS), owner.reshape(1, ROWS))
    groups, parts = PER // GROUP, len(PARTS)
    return pl.pallas_call(
        kernel,
        out_shape=jax.ShapeDtypeStruct((ROWS, PER * HEAD_DIM), BF16),
        in_specs=[hbm] * 5,
        out_specs=pl.BlockSpec(memory_space=pltpu.VMEM),
        scratch_shapes=[
            pltpu.VMEM((16, KVH * HEAD_DIM), BF16),
            pltpu.VMEM((16, KVH * HEAD_DIM), BF16),
            pltpu.VMEM((ROWS, HEAD_DIM), BF16),
            pltpu.VMEM((ROWS, PER * HEAD_DIM), BF16),
            pltpu.VMEM((SLOTS, END, ROWS), BF16),
            pltpu.VMEM((ROWS, ROWS), BF16),
            pltpu.VMEM((PER * ROWS, 2 * HEAD_DIM), BF16),
            pltpu.VMEM((PER * ROWS, ROWS), F32),
            pltpu.VMEM((PER * ROWS, ROWS), F32),
            pltpu.VMEM((PER * ROWS, HEAD_DIM), F32),
            pltpu.VMEM((N_DC * TILE, GROUP * ROWS), BF16),
            pltpu.VMEM((GROUP * ROWS, N_DC * TILE), BF16),
            pltpu.VMEM((groups, N_DC * TILE, HEAD_DIM), BF16),
            pltpu.VMEM((groups, CHIPS, 2 * TILE, HEAD_DIM), BF16),
            pltpu.VMEM((groups, CHIPS, TILE, HEAD_DIM), BF16),
            pltpu.VMEM((2, CHIPS, 1, ROWS), I32),
            pltpu.VMEM((1, N_DC * TILE), I32),
            pltpu.VMEM((1, ROWS), I32),
            pltpu.VMEM((1, ROWS), I32),
            dma((2,)), dma((2,)), dma((2,)), dma, dma, dma((COLS + 1,)), dma((2,)), dma((N_TP,)), dma, dma((2,)),
            dma((4, parts)), dma((4, parts)), dma((5, 7, parts)), dma((REACH // 2 + 1, parts)), dma((SLOTS, parts)), dma((groups,)), dma((groups,)),
            dma((groups,)), dma((groups,)), pltpu.SemaphoreType.REGULAR((3,)),
        ],
        compiler_params=pltpu.CompilerParams(
            collective_id=0, has_side_effects=True, vmem_limit_bytes=48 * 1024 * 1024
        ),
        cost_estimate=pl.CostEstimate(flops=2_300_000_000, bytes_accessed=4_000_000, transcendentals=4_500_000),
    )(*(pltpu.with_memory_space_constraint(x, pltpu.HBM) for x in operands))


def solution(mesh):
    return jax.shard_map(
        per_device,
        mesh=mesh,
        in_specs=(
            P(("dc", "tp"), None),
            P(("dc", "tp"), None),
            P(("dc", "tp"), None),
            P("dc"),
            P("dc"),
        ),
        out_specs=P("dc", "tp"),
        check_vma=False,
    )
```
